32 devices in a mesh: head: 1, blk: 32 (over z, y, x, core).
Axes of the slice: x: 2, y: 2, z: 4, core: 2. Of those that a mesh axis runs over, the one named last changes fastest.
Arguments:
- vision: bfloat16 [4, 1408, 2048], P(None, 'head', 'blk'), may hold values from -600 to 600
- ln_gain: float32 [1408], P('head'), may hold values from 0.5 to 1.5
- merge_proj: bfloat16 [4, 1408, 1408], P(None, 'head'), may hold values from -0.078125 to 0.078125
- image_slot: int32 [512], P('blk'), may hold values from 0 to 16380, as said below
- text: bfloat16 [1408, 16384], P('head', 'blk'), may hold values from -600 to 600
- rms_gain: float32 [1408], replicated, may hold values from 0.5 to 1.5
- wqkv: bfloat16 [3, 1408, 1408], P(None, 'head'), may hold values from -0.31835938 to 0.31835938
- pcache: bfloat16 [2, 1408, 65536], P(None, 'head', 'blk'), may hold values from -300 to 300
- block_table: int32 [32, 128], replicated, may hold values from -1 to 2047, as said below
- cache_len: int32 [32], P('blk'), may hold values from 1 to 4096, as said below
Outputs:
- attended: bfloat16 [1408, 16384], P('head', 'blk')
- new_cache: bfloat16 [2, 1408, 16384], P(None, 'head', 'blk')
The draws below stay inside these ranges and needn't reach their ends.
Inputs may be any that keep to these rules, and one draw needn't show every extreme that they name: `image_slot`: pieces never intersect and start at multiples of 4; the 16 pieces held by one index of blk start in the rows of 16 different requests, and every request receives exactly 16 pieces. `block_table`: row r holds a block number for j < ceil(cache_len[r] / 32) and -1 after; no block number appears twice; index d of blk holds blocks d * 64 to (d+1) * 64 - 1. The longest request has exactly 4 blocks on every index of blk; every other request has at most one block on any index. `cache_len`: exactly one request, the longest, has 4096 cached positions; all others have fewer.
All inputs are finite; a program needn't handle non-finite values.
Results may differ from the reference program's by a relative error of at most 0.025.
The reference program's roundings to bfloat16 on the way count: a program that leaves them out, or rounds other values in their place, can miss the bound.
Values may be sent and summed in bfloat16 or wider, within the bound.
No kernel may reach another device: no remote copies, remote signals or barrier semaphores. Data moves between devices by JAX's collectives and lax.ppermute only.
A program may use at most 320 MiB of HBM per device.

```python
import math
import jax
import jax.numpy as jnp
from jax import lax

D = 1408
HD = 88
PIECE = 4
BS = 32
PT_DEV = 512
BLK_DEV = 64
IMG_DEV = 16
VT = 8192
REQS = 32
NEW = 16384
MAXB = 128
TOTB = 872
NPHYS = 2048


def scaled_rows(key, rows):
    keys = jax.random.split(key, 3)
    columns = jnp.exp(jnp.arange(D, dtype=jnp.float32) * (math.log(3.0) / D))
    columns = columns * jnp.exp(math.log(3.3) * jax.random.uniform(keys[1], (D,), dtype=jnp.float32))
    row_scale = jnp.exp(math.log(10.0) * jax.random.uniform(keys[2], (rows, 1), dtype=jnp.float32))
    base = jax.random.normal(keys[0], (rows, D), dtype=jnp.float32)
    return (jnp.clip(base, -5.0, 5.0) * columns * row_scale).astype(jnp.bfloat16)


def draw_vision(key, part):
    rows = scaled_rows(jax.random.fold_in(key, 3), VT)
    return jnp.transpose(rows.reshape(VT // 4, 4, D), (1, 2, 0))


def draw_text(key, part):
    return jnp.transpose(scaled_rows(jax.random.fold_in(key, 5), NEW))


def draw_pcache(key, part):
    keys = jax.random.split(jax.random.fold_in(key, 7), 1)
    shape = (NPHYS, BS, 2, D)
    base = jnp.clip(2.0 * jax.random.normal(keys[0], shape, dtype=jnp.float32), -12.0, 12.0)
    return jnp.transpose(base.astype(jnp.bfloat16), (2, 3, 0, 1)).reshape(2, D, NPHYS * BS)


def draw_image_slot(key, part):
    keys = jax.random.split(jax.random.fold_in(key, 11), 4)
    count = REQS
    shuffle_a = jax.random.permutation(keys[0], count)
    shuffle_b = jax.random.permutation(keys[1], count)
    shifts = jax.random.permutation(keys[2], count)[:IMG_DEV]
    target = shuffle_b[(shuffle_a[:, None] + shifts[None, :]) % count]
    slots = PT_DEV // PIECE

    def order_for(device):
        return jax.random.permutation(jax.random.fold_in(keys[3], device), slots)[:IMG_DEV]
    orders = jax.vmap(order_for)(jnp.arange(count))
    chosen = orders[target, jnp.arange(IMG_DEV)[None, :]]
    return (target * PT_DEV + chosen * PIECE).reshape(-1).astype(jnp.int32)


def block_plan(key):
    keys = jax.random.split(jax.random.fold_in(key, 29), 5)
    count = REQS
    idents = jnp.arange(count)
    longest = jax.random.randint(keys[0], (), 0, count)
    others = idents != longest
    shares = jnp.where(others, jax.random.randint(keys[1], (count,), 4, 6), 0)
    spare_blocks = TOTB - MAXB - (count - 1)
    extra = spare_blocks * shares // jnp.sum(shares)
    leftover = spare_blocks - jnp.sum(extra)
    standing = jnp.cumsum(others.astype(jnp.int32)) - 1
    extra = extra + jnp.where(others & (standing < leftover), 1, 0)
    nblocks = jnp.where(others, 1 + extra, MAXB)
    tails = jax.random.randint(keys[2], (count,), 1, BS + 1)
    lengths = (nblocks - 1) * BS + jnp.where(others, tails, BS)
    begins = jnp.cumsum(nblocks) - nblocks
    shuffle_dev = jax.random.permutation(keys[3], count)

    def slots_for(device):
        return jax.random.permutation(jax.random.fold_in(keys[4], device), BLK_DEV)
    local_slots = jax.vmap(slots_for)(idents)
    columns = jnp.arange(MAXB)
    running = begins[:, None] + columns[None, :]
    device = shuffle_dev[running % count]
    layer = jnp.minimum(running // count, BLK_DEV - 1)
    physical = device * BLK_DEV + local_slots[device, layer]
    table = jnp.where(columns[None, :] < nblocks[:, None], physical, -1)
    return (table.astype(jnp.int32), lengths.astype(jnp.int32))


def draw_block_table(key, part):
    return block_plan(key)[0]


def draw_cache_len(key, part):
    return block_plan(key)[1]


def centred(key, extent, scale, most, held_as=jnp.bfloat16):
    drawn = jax.random.normal(key, extent, jnp.float32) * scale
    return jnp.minimum(jnp.maximum(drawn, -most), most).astype(held_as)


def setup_inputs(seed: int = 0) -> dict:
    streams_of = jax.random.split(jax.random.key(seed), 11)
    vision = draw_vision(jax.random.fold_in(streams_of[10], 71), 0)
    ln_gain = jnp.clip(1.0 + 0.1 * jax.random.normal(streams_of[1], (D,), jnp.float32), 0.5, 1.5)
    merge_proj = centred(streams_of[2], (4, D, D), (4 * D) ** -0.5, 0.078125)
    image_slot = draw_image_slot(jax.random.fold_in(streams_of[10], 71), 0)
    text = draw_text(jax.random.fold_in(streams_of[10], 71), 0)
    rms_gain = jnp.clip(1.0 + 0.1 * jax.random.normal(streams_of[5], (D,), jnp.float32), 0.5, 1.5)
    wqkv = centred(streams_of[6], (3, D, D), 0.0533, 0.31835938)
    pcache = draw_pcache(jax.random.fold_in(streams_of[10], 71), 0)
    block_table = draw_block_table(jax.random.fold_in(streams_of[10], 71), 0)
    cache_len = draw_cache_len(jax.random.fold_in(streams_of[10], 71), 0)
    return {"vision": vision, "ln_gain": ln_gain, "merge_proj": merge_proj, "image_slot": image_slot, "text": text, "rms_gain": rms_gain, "wqkv": wqkv, "pcache": pcache, "block_table": block_table, "cache_len": cache_len}


masked_score = -1e+30

def rotary(values, places):
    half = values.shape[-1] // 2
    freq_index = jnp.arange(half, dtype=jnp.float32)
    inverse = jnp.exp(freq_index * (-2.0 * math.log(10000.0) / values.shape[-1]))
    angles = places[:, None] * inverse[None, :]
    cosine = jnp.cos(angles)[:, None, :]
    sine_part = jnp.sin(angles)[:, None, :]
    leading = values[..., :half]
    trailing = values[..., half:]
    return jnp.concatenate([leading * cosine - trailing * sine_part, trailing * cosine + leading * sine_part], axis=-1)

def reference(vision, ln_gain, merge_proj, image_slot, text, rms_gain, wqkv, pcache, block_table, cache_len):
    width = vision.shape[1]
    groups = vision.shape[2]
    vision_rows = jnp.transpose(vision, (2, 0, 1)).reshape(groups * 4, width)
    text_rows = jnp.transpose(text)
    weight_rows = jnp.transpose(wqkv, (2, 0, 1))
    floats = vision_rows.astype(jnp.float32)
    average = lax.optimization_barrier(jnp.sum(floats, axis=1)) / width
    spread = lax.optimization_barrier(jnp.sum(floats * floats, axis=1)) / width - average * average
    normed_vision = ((floats - average[:, None]) * lax.rsqrt(spread + 1e-06)[:, None] * ln_gain).astype(jnp.bfloat16)
    merged = jnp.dot(normed_vision.reshape(groups, 4 * width), merge_proj.reshape(4 * width, width), preferred_element_type=jnp.float32).astype(jnp.bfloat16)
    piece_rows = groups // image_slot.shape[0]
    targets = (image_slot[:, None] + jnp.arange(piece_rows, dtype=jnp.int32)[None, :]).reshape(-1).astype(jnp.int32)
    placed = text_rows.at[targets].set(merged)
    row_floats = placed.astype(jnp.float32)
    mean_square = lax.optimization_barrier(jnp.sum(row_floats * row_floats, axis=1)) / width
    normed = (row_floats * lax.rsqrt(mean_square + 1e-06)[:, None] * rms_gain).astype(jnp.bfloat16)
    projected = jnp.dot(normed, weight_rows.reshape(width, 3 * width), preferred_element_type=jnp.float32)
    total_rows = text_rows.shape[0]
    requests = cache_len.shape[0]
    per_request = total_rows // requests
    head_size = HD
    heads = width // head_size
    projected = projected.reshape(total_rows, 3, heads, head_size)
    places = (jnp.repeat(cache_len, per_request) + jnp.tile(jnp.arange(per_request, dtype=jnp.int32), requests)).astype(jnp.float32)
    queries = rotary(projected[:, 0], places).astype(jnp.bfloat16)
    new_keys = rotary(projected[:, 1], places).astype(jnp.bfloat16)
    new_values = projected[:, 2].astype(jnp.bfloat16)
    new_cache = jnp.stack([new_keys.reshape(total_rows, width), new_values.reshape(total_rows, width)], axis=1)
    block_len = BS
    physical = pcache.shape[2] // block_len
    paged = pcache.reshape(2, width, physical, block_len)
    table_width = block_table.shape[1]
    scale = head_size ** (-0.5)
    lines = jnp.arange(per_request, dtype=jnp.int32)
    causal = lines[:, None] >= lines[None, :]

    def one_request(inputs):
        query_rows, key_rows, value_rows, table_row, length = inputs
        blocks = paged[:, :, jnp.clip(table_row, 0, physical - 1).astype(jnp.int32), :]
        cached_keys = jnp.transpose(blocks[0].reshape(width, table_width * block_len)).reshape(table_width * block_len, heads, head_size).astype(jnp.float32)
        cached_values = jnp.transpose(blocks[1].reshape(width, table_width * block_len)).reshape(table_width * block_len, heads, head_size).astype(jnp.float32)
        live = jnp.arange(table_width * block_len, dtype=jnp.int32) < length
        query_floats = query_rows.astype(jnp.float32)
        old_scores = jnp.einsum('qhd,khd->hqk', query_floats, cached_keys) * scale
        own_scores = jnp.einsum('qhd,khd->hqk', query_floats, key_rows.astype(jnp.float32)) * scale
        old_scores = jnp.where(live[None, None, :], old_scores, masked_score)
        own_scores = jnp.where(causal[None], own_scores, masked_score)
        highest = jnp.maximum(lax.optimization_barrier(jnp.max(old_scores, axis=2)), lax.optimization_barrier(jnp.max(own_scores, axis=2)))
        old_exp = jnp.exp(old_scores - highest[:, :, None])
        own_exp = jnp.exp(own_scores - highest[:, :, None])
        total = lax.optimization_barrier(jnp.sum(old_exp, axis=2)) + lax.optimization_barrier(jnp.sum(own_exp, axis=2))
        old_weights = old_exp / total[:, :, None]
        own_weights = own_exp / total[:, :, None]
        mixed = jnp.einsum('hqk,khd->qhd', old_weights, cached_values, precision=lax.Precision.HIGHEST)
        mixed = mixed + jnp.einsum('hqk,khd->qhd', own_weights, value_rows.astype(jnp.float32), precision=lax.Precision.HIGHEST)
        return mixed.astype(jnp.bfloat16).reshape(per_request, width)
    attended = lax.map(one_request, (queries.reshape(requests, per_request, heads, head_size), new_keys.reshape(requests, per_request, heads, head_size), new_values.reshape(requests, per_request, heads, head_size), block_table, cache_len)).reshape(total_rows, width)
    return (jnp.transpose(attended), jnp.transpose(new_cache, (1, 2, 0)))
```

```python
import functools
import math

import jax
import jax.numpy as jnp
from jax import lax
from jax.experimental import pallas as pl
from jax.experimental.pallas import tpu as pltpu
from jax.sharding import PartitionSpec as P

D = 1408
HD = 88
BS = 32
PAIR = 2 * HD
EXT = PAIR + 16
LANES = 128
MASKED = -1e30
VMEM = 48 * 1024 * 1024


masked_score = -1e30


def rotary_columns(values, places):
    half = values.shape[1] // 2
    freq_index = jnp.arange(half, dtype=jnp.float32)
    inverse = jnp.exp(freq_index * (-2.0 * math.log(10000.0) / values.shape[1]))
    angles = inverse[:, None] * places[None, :]
    cosine = jnp.cos(angles)[None]
    sine_part = jnp.sin(angles)[None]
    leading = values[:, :half]
    trailing = values[:, half:]
    return jnp.concatenate(
        [leading * cosine - trailing * sine_part, trailing * cosine + leading * sine_part], axis=1
    )


def softmax_part(query_block, keys, values, mask, scale):
    scores = (
        jnp.einsum("hdq,hdk->hqk", query_block, keys, preferred_element_type=jnp.float32) * scale
    )
    scores = jnp.where(mask[None], scores, masked_score)
    highest = jnp.max(scores, axis=2)
    expo = jnp.where(mask[None], jnp.exp(scores - highest[:, :, None]), 0.0)
    total = jnp.sum(expo, axis=2)
    mixed = jnp.einsum("hqk,hdk->hdq", expo, values, precision=lax.Precision.HIGHEST)
    return (mixed, highest, total)


def fold_softmax(first, second):
    mixed_a, high_a, total_a = first
    mixed_b, high_b, total_b = second
    top = jnp.maximum(high_a, high_b)
    factor_a = jnp.exp(high_a - top)
    factor_b = jnp.exp(high_b - top)
    return (
        mixed_a * factor_a[:, None, :] + mixed_b * factor_b[:, None, :],
        top,
        total_a * factor_a + total_b * factor_b,
    )


def unblock(parts):
    mixed, highest, total = parts
    heads_here = mixed.shape[1]
    mixed = jnp.transpose(mixed, (1, 2, 0, 3)).reshape(heads_here, mixed.shape[2], -1)
    highest = jnp.transpose(highest, (1, 0, 2)).reshape(heads_here, -1)
    total = jnp.transpose(total, (1, 0, 2)).reshape(heads_here, -1)
    return (mixed, highest, total)


def shards(
    vision, ln_gain, merge_proj, image_slot, text, rms_gain, wqkv, pcache, block_table, cache_len
):
    local = vision.shape[1]
    groups = vision.shape[2]
    floats = vision.astype(jnp.float32)
    totals, squares = lax.psum((jnp.sum(floats, axis=1), jnp.sum(floats * floats, axis=1)), "head")
    average = totals / D
    spread = squares / D - average * average
    normed_vision = (
        (floats - average[:, None, :])
        * lax.rsqrt(spread + 1e-06)[:, None, :]
        * ln_gain[None, :, None]
    ).astype(jnp.bfloat16)
    partial_rows = jnp.einsum(
        "tcd,tcg->dg", merge_proj, normed_vision, preferred_element_type=jnp.float32
    )
    merged_columns = lax.psum_scatter(partial_rows, "head", scatter_dimension=0, tiled=True).astype(
        jnp.bfloat16
    )
    merged = jnp.transpose(merged_columns)
    devices = lax.axis_size("blk")
    here = lax.axis_index("blk")
    rows_here = text.shape[1]
    pieces = image_slot.shape[0]
    piece_rows = groups // pieces
    lines = jnp.arange(rows_here, dtype=jnp.int32)
    offsets = jnp.arange(piece_rows, dtype=jnp.int32)
    target = image_slot // rows_here
    within = image_slot % rows_here
    select = target[None, :] == jnp.arange(devices, dtype=jnp.int32)[:, None]
    outbound = (
        jnp.dot(
            select.astype(jnp.bfloat16),
            merged.reshape(pieces, piece_rows * local),
            preferred_element_type=jnp.float32,
        )
        .astype(jnp.bfloat16)
        .reshape(devices, piece_rows, local)
    )
    starts = jnp.sum(jnp.where(select, within[None, :] + 1, 0), axis=1) - 1
    arrived, arrived_start = (
        lax.all_to_all(outbound, "blk", split_axis=0, concat_axis=0, tiled=True),
        lax.all_to_all(starts, "blk", split_axis=0, concat_axis=0, tiled=True),
    )
    row_ids = (arrived_start[:, None] + offsets[None, :]).reshape(-1)
    present = jnp.repeat(arrived_start >= 0, piece_rows)
    hits = (row_ids[:, None] == lines[None, :]) & present[:, None]
    placed_rows = jnp.einsum(
        "kl,kr->lr",
        arrived.reshape(devices * piece_rows, local),
        hits.astype(jnp.bfloat16),
        preferred_element_type=jnp.float32,
    ).astype(jnp.bfloat16)
    covered = jnp.any(hits, axis=0)
    placed = jnp.where(covered[None, :], placed_rows, text)
    row_floats = placed.astype(jnp.float32)
    square_sums = lax.psum(jnp.sum(row_floats * row_floats, axis=0), "head")
    gain_here = lax.dynamic_slice_in_dim(rms_gain, lax.axis_index("head") * local, local)
    normed = (row_floats * lax.rsqrt(square_sums / D + 1e-06)[None, :] * gain_here[:, None]).astype(
        jnp.bfloat16
    )
    projected = jnp.einsum(
        "jod,dr->jor",
        wqkv,
        lax.all_gather(normed, "head", axis=0, tiled=True),
        preferred_element_type=jnp.float32,
    )
    heads_here = local // HD
    projected = projected.reshape(3, heads_here, HD, rows_here)
    places = (cache_len[0] + lines).astype(jnp.float32)
    queries = rotary_columns(projected[0], places).astype(jnp.bfloat16)
    new_keys = rotary_columns(projected[1], places).astype(jnp.bfloat16)
    new_values = projected[2].astype(jnp.bfloat16)
    new_cache = jnp.stack(
        [new_keys.reshape(local, rows_here), new_values.reshape(local, rows_here)], axis=0
    )
    block_len = BS
    owned = pcache.shape[2] // block_len
    paged = pcache.reshape(2, local, owned, block_len)
    requests = block_table.shape[0]
    table_width = block_table.shape[1]
    slots_each = table_width // devices
    block_ids = here * owned + jnp.arange(owned, dtype=jnp.int32)
    matches = block_table[None, :, :] == block_ids[:, None, None]
    found = jnp.any(matches, axis=2)
    in_use = jnp.any(found, axis=1)
    owner = jnp.sum(jnp.where(found, jnp.arange(requests, dtype=jnp.int32)[None, :], 0), axis=1)
    logical = jnp.sum(
        jnp.where(matches, jnp.arange(table_width, dtype=jnp.int32)[None, None, :], 0), axis=(1, 2)
    )
    counter = jnp.arange(owned, dtype=jnp.int32)
    earlier = (
        (owner[:, None] == owner[None, :]) & in_use[None, :] & (counter[None, :] < counter[:, None])
    )
    standing = jnp.sum(earlier.astype(jnp.int32), axis=1)
    within_block = jnp.arange(block_len, dtype=jnp.int32)
    block_rows = min(rows_here, 512)
    count_blocks = rows_here // block_rows
    scale = HD ** (-0.5)
    query_blocks = jnp.transpose(
        queries.reshape(heads_here, HD, count_blocks, block_rows), (2, 0, 1, 3)
    )
    first_rows = jnp.arange(count_blocks, dtype=jnp.int32) * block_rows
    destination = owner * slots_each + standing
    routing = (destination[None, :] == jnp.arange(table_width, dtype=jnp.int32)[:, None]) & in_use[
        None, :
    ]
    outgoing = jnp.einsum(
        "wo,cfob->cfwb", routing.astype(jnp.bfloat16), paged, preferred_element_type=jnp.float32
    ).astype(jnp.bfloat16)
    outgoing = outgoing.reshape(2, local, table_width * block_len)
    labels = jnp.sum(jnp.where(routing, logical[None, :] + 1, 0), axis=1) - 1
    labels = labels.reshape(1, 1, table_width)
    blocks_in, labels_in = (
        lax.all_to_all(outgoing, "blk", split_axis=2, concat_axis=2, tiled=True),
        lax.all_to_all(labels, "blk", split_axis=2, concat_axis=2, tiled=True),
    )
    cached_keys = blocks_in[0].reshape(heads_here, HD, -1)
    cached_values = blocks_in[1].reshape(heads_here, HD, -1).astype(jnp.float32)
    label_flat = labels_in.reshape(-1)
    key_places = label_flat[:, None] * block_len + within_block[None, :]
    live = ((label_flat[:, None] >= 0) & (key_places < cache_len[0])).reshape(-1)
    old_mask = jnp.broadcast_to(live[None, :], (block_rows, live.shape[0]))
    new_values_f = new_values.astype(jnp.float32)

    def attend(inputs):
        query_block, first_row = inputs
        causal = (first_row + jnp.arange(block_rows, dtype=jnp.int32))[:, None] >= lines[None, :]
        old_part = softmax_part(query_block, cached_keys, cached_values, old_mask, scale)
        own_part = softmax_part(query_block, new_keys, new_values_f, causal, scale)
        return fold_softmax(old_part, own_part)

    mixed, highest, total = unblock(lax.map(attend, (query_blocks, first_rows)))
    attended = (mixed / total[:, None, :]).astype(jnp.bfloat16).reshape(local, rows_here)
    return (attended, new_cache)


def pack_body(ids, cache_ref, out_ref, *, slots):
    lane = lax.broadcasted_iota(jnp.int32, (PAIR, LANES), 1) // BS

    def one(w, carry):
        block = ids[w]
        start = pl.multiple_of(block // 4 * LANES, LANES)
        turn = block % 4
        packed = None
        for g in range(4):
            tile = cache_ref[g // 2, g % 2, :, pl.ds(start, LANES)]
            tile = pltpu.roll(tile, (g + 4 - turn) % 4 * BS, 1)
            packed = tile if g == 0 else jnp.where(lane == g, tile, packed)
        out_ref[w] = packed
        return carry

    lax.fori_loop(0, slots, one, 0, unroll=2)


def pack_unit(ids, paged, unit):
    slots = ids.shape[0]
    lanes = paged.shape[3]
    return pl.pallas_call(
        functools.partial(pack_body, slots=slots),
        grid_spec=pltpu.PrefetchScalarGridSpec(
            num_scalar_prefetch=1,
            grid=(1,),
            in_specs=[pl.BlockSpec((2, 2, PAIR, lanes), lambda i, s: (0, unit, 0, 0))],
            out_specs=pl.BlockSpec((slots, PAIR, LANES), lambda i, s: (0, 0, 0)),
        ),
        out_shape=jax.ShapeDtypeStruct((slots, PAIR, LANES), jnp.bfloat16),
        compiler_params=pltpu.CompilerParams(vmem_limit_bytes=VMEM),
        cost_estimate=pl.CostEstimate(flops=0, bytes_accessed=4500000, transcendentals=0),
        name="pack_blocks",
    )(ids, paged)


def star_pack_body(ids, *refs):
    out_ref = refs[8]
    lane = lax.broadcasted_iota(jnp.int32, (PAIR, LANES), 1) // BS
    for c in range(2):
        packed = None
        for j in range(4):
            tile = pltpu.roll(refs[c * 4 + j][0, 0], (j + 4 - ids[j] % 4) % 4 * BS, 1)
            packed = tile if j == 0 else jnp.where(lane == j, tile, packed)
        out_ref[0, c] = packed


def star_pack(ids, paged):
    pairs = paged.shape[1]

    def spec(c, j):
        return pl.BlockSpec((1, 1, PAIR, LANES), lambda i, s: (c, pair_of(i), 0, s[j] // 4))

    return pl.pallas_call(
        star_pack_body,
        grid_spec=pltpu.PrefetchScalarGridSpec(
            num_scalar_prefetch=1,
            grid=(pairs,),
            in_specs=[spec(c, j) for c in range(2) for j in range(4)],
            out_specs=pl.BlockSpec((1, 2, PAIR, LANES), lambda i, s: (i, 0, 0, 0)),
        ),
        out_shape=jax.ShapeDtypeStruct((pairs, 2, PAIR, LANES), jnp.bfloat16),
        compiler_params=pltpu.CompilerParams(vmem_limit_bytes=VMEM),
        name="pack_longest",
    )(ids, *([paged] * 8))


def pair_of(place):
    return place % 2 * 4 + place // 2 % 2 * 2 + place // 4


def project_body(normed_ref, weight_ref, cos_ref, sin_ref, query_ref, cache_ref):
    normed = normed_ref[...]

    def part(j):
        return jnp.dot(weight_ref[j], normed, preferred_element_type=jnp.float32)

    def rotate(x):
        heads = []
        for h in range(2):
            one = x[h * HD : (h + 1) * HD]
            other = jnp.concatenate([one[HD // 2 :], one[: HD // 2]], axis=0)
            heads.append(one * cos_ref[...] + other * sin_ref[...])
        return jnp.concatenate(heads, axis=0).astype(jnp.bfloat16)

    query_ref[0] = rotate(part(0))
    cache_ref[0] = rotate(part(1))
    cache_ref[1] = part(2).astype(jnp.bfloat16)


def project(normed, wqkv, cosine, sine):
    width, rows = normed.shape
    pairs = width // PAIR
    return pl.pallas_call(
        project_body,
        grid=(pairs,),
        in_specs=[
            pl.BlockSpec((width, rows), lambda i: (0, 0)),
            pl.BlockSpec((3, PAIR, width), lambda i: (0, i, 0)),
            pl.BlockSpec((HD, rows), lambda i: (0, 0)),
            pl.BlockSpec((HD, rows), lambda i: (0, 0)),
        ],
        out_specs=[
            pl.BlockSpec((1, PAIR, rows), lambda i: (i, 0, 0)),
            pl.BlockSpec((2, PAIR, rows), lambda i: (0, i, 0)),
        ],
        out_shape=[
            jax.ShapeDtypeStruct((pairs, PAIR, rows), jnp.bfloat16),
            jax.ShapeDtypeStruct((2, width, rows), jnp.bfloat16),
        ],
        compiler_params=pltpu.CompilerParams(vmem_limit_bytes=VMEM),
        cost_estimate=pl.CostEstimate(
            flops=6 * width * width * rows, bytes_accessed=8 * width * width, transcendentals=0
        ),
        name="project_rotate",
    )(normed, wqkv, cosine, sine)


def split_three(x):
    high = x.astype(jnp.bfloat16).astype(jnp.float32)
    middle = (x - high).astype(jnp.bfloat16).astype(jnp.float32)
    return high, middle, x - high - middle


def attend_pair(query, keys, values, old, own, out):
    rows = query.shape[1]
    step = min(256, rows)
    extra = jnp.where(lax.broadcasted_iota(jnp.int32, (EXT - PAIR, rows), 0) == 0, 1.0, 0.0)
    turned = jnp.transpose(jnp.concatenate([query, extra.astype(jnp.bfloat16)], axis=0))
    column = lax.broadcasted_iota(jnp.int32, (step, EXT), 1)
    ahead = lax.broadcasted_iota(jnp.int32, (step, step), 1) > lax.broadcasted_iota(jnp.int32, (step, step), 0)
    factor = math.log2(math.e) * HD ** (-0.5)
    for first in range(0, rows, step):
        count = old + (first + step if own else 0)
        parts = []
        for h in range(2):
            used = (column // HD == h) | (column == PAIR)
            mine = jnp.where(used, turned[first : first + step], 0).astype(jnp.bfloat16)
            scores = jnp.dot(mine, keys[:, :count], preferred_element_type=jnp.float32)
            if own:
                last = jnp.where(ahead, MASKED, scores[:, count - step :])
                scores = jnp.concatenate([scores[:, : count - step], last], axis=1)
            highest = jnp.max(scores, axis=1, keepdims=True)
            expo = jnp.exp2((scores - highest) * factor).astype(jnp.bfloat16)
            mixed = lax.dot_general(
                expo, values[:, :count], (((1,), (1,)), ((), ())), preferred_element_type=jnp.float32
            )
            total = mixed[:, PAIR : PAIR + 1]
            parts.append((mixed / total, split_three(highest * factor + jnp.log2(total))))
        result = jnp.where(column < HD, parts[0][0], parts[1][0])
        for h in range(2):
            for j in range(3):
                result = jnp.where(column == PAIR + 2 * j + h, parts[h][1][j], result)
        result = jnp.where(column >= PAIR + 6, 0.0, result)
        out[:, first : first + step] = jnp.transpose(result).astype(jnp.bfloat16)


def attend_body(arrived_ref, bias_ref, query_ref, own_ref, out_ref, kv, *, own_rows):
    old = bias_ref.shape[1]
    lower = lax.broadcasted_iota(jnp.int32, (EXT - PAIR, old + own_rows), 0)
    masks = jnp.concatenate([bias_ref[...], jnp.zeros((1, own_rows), jnp.float32)], axis=1)
    for g in range(2):
        kv[g, PAIR:EXT] = jnp.where(lower == 0, masks, 0.0).astype(jnp.bfloat16)
        kv[2 + g, PAIR:EXT] = jnp.where(lower == 0, 1.0, 0.0).astype(jnp.bfloat16)
        kv[g, 0:PAIR, old:] = own_ref[0, g * PAIR : (g + 1) * PAIR]
        kv[2 + g, 0:PAIR, old:] = own_ref[1, g * PAIR : (g + 1) * PAIR]
    for t in range(old // LANES):
        tiles = [arrived_ref[4 * t + j] for j in range(4)]
        for g in range(4):
            kv[g, 0:PAIR, t * LANES : (t + 1) * LANES] = jnp.concatenate(
                [tile[:, g * BS : (g + 1) * BS] for tile in tiles], axis=1
            )
    for g in range(2):
        attend_pair(query_ref[g], kv.at[g], kv.at[2 + g], old, True, out_ref.at[g])


def attend_unit(arrived, bias, queries, new_cache, unit):
    rows = queries.shape[2]
    old = bias.shape[1]
    work = 4 * rows * (old + rows)
    return pl.pallas_call(
        functools.partial(attend_body, own_rows=rows),
        grid=(1,),
        in_specs=[
            pl.BlockSpec(arrived.shape, lambda i: (0, 0, 0)),
            pl.BlockSpec((1, old), lambda i: (0, 0)),
            pl.BlockSpec((2, PAIR, rows), lambda i: (unit, 0, 0)),
            pl.BlockSpec((2, 2 * PAIR, rows), lambda i: (0, unit, 0)),
        ],
        out_specs=pl.BlockSpec((2, EXT, rows), lambda i: (0, 0, 0)),
        out_shape=jax.ShapeDtypeStruct((2, EXT, rows), jnp.bfloat16),
        scratch_shapes=[pltpu.VMEM((4, EXT, old + rows), jnp.bfloat16)],
        compiler_params=pltpu.CompilerParams(vmem_limit_bytes=VMEM),
        cost_estimate=pl.CostEstimate(
            flops=work * 1024, bytes_accessed=4000000, transcendentals=work
        ),
        name="attend_heads",
    )(arrived, bias, queries, new_cache)


def star_body(arrived_ref, query_ref, out_ref, kv, *, sources):
    lower = lax.broadcasted_iota(jnp.int32, (EXT - PAIR, sources * LANES), 0)
    kv[0, PAIR:EXT] = jnp.zeros(lower.shape, jnp.bfloat16)
    kv[1, PAIR:EXT] = jnp.where(lower == 0, 1.0, 0.0).astype(jnp.bfloat16)
    for s in range(sources):
        for c in range(2):
            kv[c, 0:PAIR, s * LANES : (s + 1) * LANES] = arrived_ref[s, c]
    attend_pair(query_ref[...], kv.at[0], kv.at[1], sources * LANES, False, out_ref)


def star_attend(arrived, query):
    sources = arrived.shape[0]
    rows = query.shape[1]
    work = 2 * rows * sources * LANES
    return pl.pallas_call(
        functools.partial(star_body, sources=sources),
        out_shape=jax.ShapeDtypeStruct((EXT, rows), jnp.bfloat16),
        scratch_shapes=[pltpu.VMEM((2, EXT, sources * LANES), jnp.bfloat16)],
        compiler_params=pltpu.CompilerParams(vmem_limit_bytes=VMEM),
        cost_estimate=pl.CostEstimate(
            flops=work * 1024, bytes_accessed=1500000, transcendentals=work
        ),
        name="attend_longest",
    )(arrived, query)


def fold_two(first, second):
    def logs(x):
        return [x[PAIR + h : PAIR + h + 1] + x[PAIR + 2 + h : PAIR + 3 + h] + x[PAIR + 4 + h : PAIR + 5 + h] for h in range(2)]

    logs_a, logs_b = logs(first), logs(second)
    heads, below = [], []
    for h in range(2):
        top = jnp.maximum(logs_a[h], logs_b[h])
        share_a, share_b = jnp.exp2(logs_a[h] - top), jnp.exp2(logs_b[h] - top)
        total = share_a + share_b
        span = slice(h * HD, (h + 1) * HD)
        heads.append((first[span] * share_a + second[span] * share_b) / total)
        below.append(split_three(top + jnp.log2(total)))
    return heads, below


def fold_body(first_ref, second_ref, out_ref):
    heads, below = fold_two(first_ref[...].astype(jnp.float32), second_ref[...].astype(jnp.float32))
    row = lax.broadcasted_iota(jnp.int32, (EXT - PAIR, out_ref.shape[1]), 0)
    lower = jnp.zeros(row.shape, jnp.float32)
    for j in range(3):
        for h in range(2):
            lower = jnp.where(row == 2 * j + h, below[h][j], lower)
    out_ref[...] = jnp.concatenate(heads + [lower], axis=0).astype(jnp.bfloat16)


def fold(first, second):
    return pl.pallas_call(
        fold_body,
        out_shape=jax.ShapeDtypeStruct(first.shape, jnp.bfloat16),
        compiler_params=pltpu.CompilerParams(vmem_limit_bytes=VMEM),
        name="fold_parts",
    )(first, second)


def finish_body(flag, star_ref, *refs):
    out_ref = refs[-1]
    for u, unit_ref in enumerate(refs[:-1]):
        for g in range(2):
            pair = 2 * u + g
            span = pl.ds(pair * PAIR, PAIR)
            out_ref[span] = unit_ref[g, 0:PAIR]

            @pl.when(flag[0] == 1)
            def _():
                heads, _ = fold_two(unit_ref[g].astype(jnp.float32), star_ref[pair].astype(jnp.float32))
                out_ref[span] = jnp.concatenate(heads, axis=0).astype(jnp.bfloat16)


def finish(flag, star, units):
    pairs, _, rows = star.shape
    whole = [pl.BlockSpec(star.shape, lambda i, s: (0, 0, 0))]
    return pl.pallas_call(
        finish_body,
        grid_spec=pltpu.PrefetchScalarGridSpec(
            num_scalar_prefetch=1,
            grid=(1,),
            in_specs=whole + [pl.BlockSpec(u.shape, lambda i, s: (0, 0, 0)) for u in units],
            out_specs=pl.BlockSpec((pairs * PAIR, rows), lambda i, s: (0, 0)),
        ),
        out_shape=jax.ShapeDtypeStruct((pairs * PAIR, rows), jnp.bfloat16),
        compiler_params=pltpu.CompilerParams(vmem_limit_bytes=VMEM),
        name="finish_heads",
    )(flag, star, *units)


def place_and_norm(vision, ln_gain, merge_proj, image_slot, text, rms_gain):
    groups = vision.shape[2]
    width = vision.shape[1]
    floats = vision.astype(jnp.float32)
    average = jnp.sum(floats, axis=1) / D
    spread = jnp.sum(floats * floats, axis=1) / D - average * average
    normed_vision = (
        (floats - average[:, None, :])
        * lax.rsqrt(spread + 1e-06)[:, None, :]
        * ln_gain[None, :, None]
    ).astype(jnp.bfloat16)
    merged = jnp.einsum(
        "tcd,tcg->gd", merge_proj, normed_vision, preferred_element_type=jnp.float32
    ).astype(jnp.bfloat16)
    devices = lax.axis_size("blk")
    rows_here = text.shape[1]
    pieces = image_slot.shape[0]
    piece_rows = groups // pieces
    lines = jnp.arange(rows_here, dtype=jnp.int32)
    offsets = jnp.arange(piece_rows, dtype=jnp.int32)
    target = image_slot // rows_here
    within = image_slot % rows_here
    select = target[None, :] == jnp.arange(devices, dtype=jnp.int32)[:, None]
    outbound = (
        jnp.dot(
            select.astype(jnp.bfloat16),
            merged.reshape(pieces, piece_rows * width),
            preferred_element_type=jnp.float32,
        )
        .astype(jnp.bfloat16)
        .reshape(devices, piece_rows, width)
    )
    starts = jnp.sum(jnp.where(select, within[None, :] + 1, 0), axis=1) - 1
    arrived = lax.all_to_all(outbound, "blk", split_axis=0, concat_axis=0, tiled=True)
    arrived_start = lax.all_to_all(starts, "blk", split_axis=0, concat_axis=0, tiled=True)
    row_ids = (arrived_start[:, None] + offsets[None, :]).reshape(-1)
    present = jnp.repeat(arrived_start >= 0, piece_rows)
    hits = (row_ids[:, None] == lines[None, :]) & present[:, None]
    placed_rows = jnp.einsum(
        "kl,kr->lr",
        arrived.reshape(devices * piece_rows, width),
        hits.astype(jnp.bfloat16),
        preferred_element_type=jnp.float32,
    ).astype(jnp.bfloat16)
    covered = jnp.any(hits, axis=0)
    placed = jnp.where(covered[None, :], placed_rows, text)
    row_floats = placed.astype(jnp.float32)
    square_sums = jnp.sum(row_floats * row_floats, axis=0)
    return (row_floats * lax.rsqrt(square_sums / D + 1e-06)[None, :] * rms_gain[:, None]).astype(
        jnp.bfloat16
    )


def rotary_tables(places):
    half = HD // 2
    freq_index = jnp.arange(half, dtype=jnp.float32)
    inverse = jnp.exp(freq_index * (-2.0 * math.log(10000.0) / HD))
    angles = inverse[:, None] * places[None, :]
    cosine = jnp.cos(angles)
    sine = jnp.sin(angles)
    return jnp.concatenate([cosine, cosine], axis=0), jnp.concatenate([-sine, sine], axis=0)


def swap(x, bit):
    size = lax.axis_size("blk")
    return lax.ppermute(x, "blk", [(i, i ^ (1 << bit)) for i in range(size)])


def spread_shards(
    vision, ln_gain, merge_proj, image_slot, text, rms_gain, wqkv, pcache, block_table, cache_len
):
    devices = lax.axis_size("blk")
    here = lax.axis_index("blk")
    width, rows = text.shape
    pairs = width // PAIR
    owned = pcache.shape[2] // BS
    table_width = block_table.shape[1]
    each = table_width // devices

    holder = jnp.where(block_table >= 0, block_table // owned, -1)
    local = block_table - here * owned
    mine = holder == here
    longest = jnp.argmax(block_table[:, table_width - 1]).astype(jnp.int32)
    chosen = jnp.max(jnp.where(mine, local, 0), axis=1)
    star_row = jnp.where(
        lax.dynamic_index_in_dim(mine, longest, 0, False),
        lax.dynamic_index_in_dim(local, longest, 0, False),
        -1,
    )
    rank = jnp.sum((star_row[None, :] > star_row[:, None]).astype(jnp.int32), axis=1)
    star_ids = jnp.sum(
        jnp.where(
            (rank[None, :] == jnp.arange(each, dtype=jnp.int32)[:, None]) & (star_row >= 0)[None, :],
            star_row[None, :],
            0,
        ),
        axis=1,
    )
    row_holder = lax.dynamic_index_in_dim(holder, here, 0, False)
    row_count = jnp.clip(cache_len[0] - BS * jnp.arange(table_width, dtype=jnp.int32), 0, BS)
    live = jnp.sum(
        jnp.where(
            row_holder[None, :] == jnp.arange(devices, dtype=jnp.int32)[:, None], row_count[None, :], 0
        ),
        axis=1,
    )
    live = jnp.where(here == longest, 0, live)
    bias = jnp.where(jnp.arange(BS, dtype=jnp.int32)[None, :] < live[:, None], 0.0, MASKED)
    bias = bias.astype(jnp.float32).reshape(1, devices * BS)

    paged = pcache.reshape(2, pairs, PAIR, owned * BS)
    units = pairs // 2
    planes = [[p * pairs + i for i in range(pairs)] for p in range(devices // pairs)]

    def exchange(x, groups=None):
        return lax.all_to_all(x, "blk", split_axis=0, concat_axis=0, tiled=True, axis_index_groups=groups)

    arrived = []
    for u in range(units):
        arrived.append(exchange(pack_unit(chosen, paged, u)))
    star_kv = exchange(star_pack(star_ids, paged), planes)

    normed = place_and_norm(vision, ln_gain, merge_proj, image_slot, text, rms_gain)
    places = (cache_len[0] + jnp.arange(rows, dtype=jnp.int32)).astype(jnp.float32)
    queries, new_cache = project(normed, wqkv, *rotary_tables(places))

    query = queries
    plane_bits = pairs.bit_length() - 1
    all_bits = devices.bit_length() - 1
    for bit in range(plane_bits):
        mine_bit, star_bit = (here >> bit) & 1, (longest >> bit) & 1
        halves = query.reshape(2, query.shape[0] // 2, PAIR, rows)
        kept = lax.dynamic_index_in_dim(halves, mine_bit, 0, False)
        given = lax.dynamic_index_in_dim(halves, 1 - mine_bit, 0, False)
        query = jnp.where(star_bit == mine_bit, kept, swap(given, bit))
    for bit in range(plane_bits, all_bits):
        same = ((here ^ longest) >> bit) & 1
        query = jnp.where(same == 0, query, swap(query, bit))
    star = star_attend(star_kv, query[0])
    for bit in range(plane_bits, all_bits):
        star = fold(star, swap(star, bit))
    star = star[None]
    for bit in reversed(range(plane_bits)):
        other = swap(star, bit)
        mine_bit = (here >> bit) & 1
        star = jnp.where(
            mine_bit == 0, jnp.concatenate([star, other]), jnp.concatenate([other, star])
        )

    results = [attend_unit(arrived[u], bias, queries, new_cache, u) for u in range(units)]
    flag = (here == longest).astype(jnp.int32).reshape(1)
    return (finish(flag, star, results), new_cache)


def spreads(mesh):
    devices = mesh.shape["blk"]
    pairs = D // PAIR
    return mesh.shape["head"] == 1 and devices % pairs == 0 and devices & (devices - 1) == 0


def solution(mesh):
    in_specs = (
        P(None, "head", "blk"),
        P("head"),
        P(None, "head", None),
        P("blk"),
        P("head", "blk"),
        P(),
        P(None, "head", None),
        P(None, "head", "blk"),
        P(),
        P("blk"),
    )
    out_specs = (P("head", "blk"), P(None, "head", "blk"))
    body = spread_shards if spreads(mesh) else shards
    return jax.shard_map(body, mesh=mesh, in_specs=in_specs, out_specs=out_specs, check_vma=False)
```

```python
import functools
import math

import jax
import jax.numpy as jnp
from jax import lax
from jax.experimental import pallas as pl
from jax.experimental.pallas import tpu as pltpu
from jax.sharding import PartitionSpec as P

D = 1408
HD = 88
BS = 32
PAIR = 2 * HD
EXT = PAIR + 16
LANES = 128
MASKED = -1e30
VMEM = 60 * 1024 * 1024


masked_score = -1e30


def rotary_columns(values, places):
    half = values.shape[1] // 2
    freq_index = jnp.arange(half, dtype=jnp.float32)
    inverse = jnp.exp(freq_index * (-2.0 * math.log(10000.0) / values.shape[1]))
    angles = inverse[:, None] * places[None, :]
    cosine = jnp.cos(angles)[None]
    sine_part = jnp.sin(angles)[None]
    leading = values[:, :half]
    trailing = values[:, half:]
    return jnp.concatenate(
        [leading * cosine - trailing * sine_part, trailing * cosine + leading * sine_part], axis=1
    )


def softmax_part(query_block, keys, values, mask, scale):
    scores = (
        jnp.einsum("hdq,hdk->hqk", query_block, keys, preferred_element_type=jnp.float32) * scale
    )
    scores = jnp.where(mask[None], scores, masked_score)
    highest = jnp.max(scores, axis=2)
    expo = jnp.where(mask[None], jnp.exp(scores - highest[:, :, None]), 0.0)
    total = jnp.sum(expo, axis=2)
    mixed = jnp.einsum("hqk,hdk->hdq", expo, values, precision=lax.Precision.HIGHEST)
    return (mixed, highest, total)


def fold_softmax(first, second):
    mixed_a, high_a, total_a = first
    mixed_b, high_b, total_b = second
    top = jnp.maximum(high_a, high_b)
    factor_a = jnp.exp(high_a - top)
    factor_b = jnp.exp(high_b - top)
    return (
        mixed_a * factor_a[:, None, :] + mixed_b * factor_b[:, None, :],
        top,
        total_a * factor_a + total_b * factor_b,
    )


def unblock(parts):
    mixed, highest, total = parts
    heads_here = mixed.shape[1]
    mixed = jnp.transpose(mixed, (1, 2, 0, 3)).reshape(heads_here, mixed.shape[2], -1)
    highest = jnp.transpose(highest, (1, 0, 2)).reshape(heads_here, -1)
    total = jnp.transpose(total, (1, 0, 2)).reshape(heads_here, -1)
    return (mixed, highest, total)


def shards(
    vision, ln_gain, merge_proj, image_slot, text, rms_gain, wqkv, pcache, block_table, cache_len
):
    local = vision.shape[1]
    groups = vision.shape[2]
    floats = vision.astype(jnp.float32)
    totals, squares = lax.psum((jnp.sum(floats, axis=1), jnp.sum(floats * floats, axis=1)), "head")
    average = totals / D
    spread = squares / D - average * average
    normed_vision = (
        (floats - average[:, None, :])
        * lax.rsqrt(spread + 1e-06)[:, None, :]
        * ln_gain[None, :, None]
    ).astype(jnp.bfloat16)
    partial_rows = jnp.einsum(
        "tcd,tcg->dg", merge_proj, normed_vision, preferred_element_type=jnp.float32
    )
    merged_columns = lax.psum_scatter(partial_rows, "head", scatter_dimension=0, tiled=True).astype(
        jnp.bfloat16
    )
    merged = jnp.transpose(merged_columns)
    devices = lax.axis_size("blk")
    here = lax.axis_index("blk")
    rows_here = text.shape[1]
    pieces = image_slot.shape[0]
    piece_rows = groups // pieces
    lines = jnp.arange(rows_here, dtype=jnp.int32)
    offsets = jnp.arange(piece_rows, dtype=jnp.int32)
    target = image_slot // rows_here
    within = image_slot % rows_here
    select = target[None, :] == jnp.arange(devices, dtype=jnp.int32)[:, None]
    outbound = (
        jnp.dot(
            select.astype(jnp.bfloat16),
            merged.reshape(pieces, piece_rows * local),
            preferred_element_type=jnp.float32,
        )
        .astype(jnp.bfloat16)
        .reshape(devices, piece_rows, local)
    )
    starts = jnp.sum(jnp.where(select, within[None, :] + 1, 0), axis=1) - 1
    arrived, arrived_start = (
        lax.all_to_all(outbound, "blk", split_axis=0, concat_axis=0, tiled=True),
        lax.all_to_all(starts, "blk", split_axis=0, concat_axis=0, tiled=True),
    )
    row_ids = (arrived_start[:, None] + offsets[None, :]).reshape(-1)
    present = jnp.repeat(arrived_start >= 0, piece_rows)
    hits = (row_ids[:, None] == lines[None, :]) & present[:, None]
    placed_rows = jnp.einsum(
        "kl,kr->lr",
        arrived.reshape(devices * piece_rows, local),
        hits.astype(jnp.bfloat16),
        preferred_element_type=jnp.float32,
    ).astype(jnp.bfloat16)
    covered = jnp.any(hits, axis=0)
    placed = jnp.where(covered[None, :], placed_rows, text)
    row_floats = placed.astype(jnp.float32)
    square_sums = lax.psum(jnp.sum(row_floats * row_floats, axis=0), "head")
    gain_here = lax.dynamic_slice_in_dim(rms_gain, lax.axis_index("head") * local, local)
    normed = (row_floats * lax.rsqrt(square_sums / D + 1e-06)[None, :] * gain_here[:, None]).astype(
        jnp.bfloat16
    )
    projected = jnp.einsum(
        "jod,dr->jor",
        wqkv,
        lax.all_gather(normed, "head", axis=0, tiled=True),
        preferred_element_type=jnp.float32,
    )
    heads_here = local // HD
    projected = projected.reshape(3, heads_here, HD, rows_here)
    places = (cache_len[0] + lines).astype(jnp.float32)
    queries = rotary_columns(projected[0], places).astype(jnp.bfloat16)
    new_keys = rotary_columns(projected[1], places).astype(jnp.bfloat16)
    new_values = projected[2].astype(jnp.bfloat16)
    new_cache = jnp.stack(
        [new_keys.reshape(local, rows_here), new_values.reshape(local, rows_here)], axis=0
    )
    block_len = BS
    owned = pcache.shape[2] // block_len
    paged = pcache.reshape(2, local, owned, block_len)
    requests = block_table.shape[0]
    table_width = block_table.shape[1]
    slots_each = table_width // devices
    block_ids = here * owned + jnp.arange(owned, dtype=jnp.int32)
    matches = block_table[None, :, :] == block_ids[:, None, None]
    found = jnp.any(matches, axis=2)
    in_use = jnp.any(found, axis=1)
    owner = jnp.sum(jnp.where(found, jnp.arange(requests, dtype=jnp.int32)[None, :], 0), axis=1)
    logical = jnp.sum(
        jnp.where(matches, jnp.arange(table_width, dtype=jnp.int32)[None, None, :], 0), axis=(1, 2)
    )
    counter = jnp.arange(owned, dtype=jnp.int32)
    earlier = (
        (owner[:, None] == owner[None, :]) & in_use[None, :] & (counter[None, :] < counter[:, None])
    )
    standing = jnp.sum(earlier.astype(jnp.int32), axis=1)
    within_block = jnp.arange(block_len, dtype=jnp.int32)
    block_rows = min(rows_here, 512)
    count_blocks = rows_here // block_rows
    scale = HD ** (-0.5)
    query_blocks = jnp.transpose(
        queries.reshape(heads_here, HD, count_blocks, block_rows), (2, 0, 1, 3)
    )
    first_rows = jnp.arange(count_blocks, dtype=jnp.int32) * block_rows
    destination = owner * slots_each + standing
    routing = (destination[None, :] == jnp.arange(table_width, dtype=jnp.int32)[:, None]) & in_use[
        None, :
    ]
    outgoing = jnp.einsum(
        "wo,cfob->cfwb", routing.astype(jnp.bfloat16), paged, preferred_element_type=jnp.float32
    ).astype(jnp.bfloat16)
    outgoing = outgoing.reshape(2, local, table_width * block_len)
    labels = jnp.sum(jnp.where(routing, logical[None, :] + 1, 0), axis=1) - 1
    labels = labels.reshape(1, 1, table_width)
    blocks_in, labels_in = (
        lax.all_to_all(outgoing, "blk", split_axis=2, concat_axis=2, tiled=True),
        lax.all_to_all(labels, "blk", split_axis=2, concat_axis=2, tiled=True),
    )
    cached_keys = blocks_in[0].reshape(heads_here, HD, -1)
    cached_values = blocks_in[1].reshape(heads_here, HD, -1).astype(jnp.float32)
    label_flat = labels_in.reshape(-1)
    key_places = label_flat[:, None] * block_len + within_block[None, :]
    live = ((label_flat[:, None] >= 0) & (key_places < cache_len[0])).reshape(-1)
    old_mask = jnp.broadcast_to(live[None, :], (block_rows, live.shape[0]))
    new_values_f = new_values.astype(jnp.float32)

    def attend(inputs):
        query_block, first_row = inputs
        causal = (first_row + jnp.arange(block_rows, dtype=jnp.int32))[:, None] >= lines[None, :]
        old_part = softmax_part(query_block, cached_keys, cached_values, old_mask, scale)
        own_part = softmax_part(query_block, new_keys, new_values_f, causal, scale)
        return fold_softmax(old_part, own_part)

    mixed, highest, total = unblock(lax.map(attend, (query_blocks, first_rows)))
    attended = (mixed / total[:, None, :]).astype(jnp.bfloat16).reshape(local, rows_here)
    return (attended, new_cache)


def pack_body(ids, cache_ref, out_ref, *, slots):
    lane = lax.broadcasted_iota(jnp.int32, (PAIR, LANES), 1) // BS

    def one(w, carry):
        block = ids[w]
        start = pl.multiple_of(block // 4 * LANES, LANES)
        turn = block % 4
        packed = None
        for g in range(4):
            tile = cache_ref[g // 2, g % 2, :, pl.ds(start, LANES)]
            tile = pltpu.roll(tile, (g + 4 - turn) % 4 * BS, 1)
            packed = tile if g == 0 else jnp.where(lane == g, tile, packed)
        out_ref[w, 0] = packed
        return carry

    lax.fori_loop(0, slots, one, 0, unroll=8)


def pack_units(ids, paged, first, count):
    slots = ids.shape[0]
    lanes = paged.shape[3]
    return pl.pallas_call(
        functools.partial(pack_body, slots=slots),
        grid_spec=pltpu.PrefetchScalarGridSpec(
            num_scalar_prefetch=1,
            grid=(count,),
            in_specs=[pl.BlockSpec((2, 2, PAIR, lanes), lambda i, s: (0, first + i, 0, 0))],
            out_specs=pl.BlockSpec((slots, 1, PAIR, LANES), lambda i, s: (0, i, 0, 0)),
        ),
        out_shape=jax.ShapeDtypeStruct((slots, count, PAIR, LANES), jnp.bfloat16),
        compiler_params=pltpu.CompilerParams(vmem_limit_bytes=VMEM),
        cost_estimate=pl.CostEstimate(
            flops=0, bytes_accessed=4500000 * count, transcendentals=0
        ),
        name="pack_blocks",
    )(ids, paged)


def star_pack_body(ids, *refs):
    lane = lax.broadcasted_iota(jnp.int32, (PAIR, LANES), 1) // BS
    for c in range(2):
        packed = None
        for j in range(4):
            tile = pltpu.roll(refs[c * 4 + j][0, 0], (j + 4 - ids[1 + j] % 4) % 4 * BS, 1)
            packed = tile if j == 0 else jnp.where(lane == j, tile, packed)
        refs[8][0, c] = packed


def star_pack(ids, paged):
    pairs = paged.shape[1]

    def spec(c, j):
        return pl.BlockSpec((1, 1, PAIR, LANES), lambda i, s: (c, i ^ s[0], 0, s[1 + j] // 4))

    return pl.pallas_call(
        star_pack_body,
        grid_spec=pltpu.PrefetchScalarGridSpec(
            num_scalar_prefetch=1,
            grid=(pairs,),
            in_specs=[spec(c, j) for c in range(2) for j in range(4)],
            out_specs=pl.BlockSpec((1, 2, PAIR, LANES), lambda i, s: (i, 0, 0, 0)),
        ),
        out_shape=jax.ShapeDtypeStruct((pairs, 2, PAIR, LANES), jnp.bfloat16),
        compiler_params=pltpu.CompilerParams(vmem_limit_bytes=VMEM),
        cost_estimate=pl.CostEstimate(flops=0, bytes_accessed=4000000, transcendentals=0),
        name="pack_longest",
    )(ids, *([paged] * 8))


def rotate_heads(x, cosine, sine):
    heads = []
    for h in range(2):
        one = x[h * HD : (h + 1) * HD]
        other = jnp.concatenate([one[HD // 2 :], one[: HD // 2]], axis=0)
        heads.append(one * cosine + other * sine)
    return jnp.concatenate(heads, axis=0).astype(jnp.bfloat16)


def query_body(normed_ref, weight_ref, cos_ref, sin_ref, query_ref):
    x = jnp.dot(weight_ref[0], normed_ref[...], preferred_element_type=jnp.float32)
    for g in range(query_ref.shape[0]):
        query_ref[g] = rotate_heads(x[g * PAIR : (g + 1) * PAIR], cos_ref[...], sin_ref[...])


def cache_body(normed_ref, key_ref, value_ref, cos_ref, sin_ref, cache_ref):
    normed = normed_ref[...]
    x = jnp.dot(key_ref[0], normed, preferred_element_type=jnp.float32)
    for g in range(x.shape[0] // PAIR):
        span = slice(g * PAIR, (g + 1) * PAIR)
        cache_ref[0, span] = rotate_heads(x[span], cos_ref[...], sin_ref[...])
    x = jnp.dot(value_ref[0], normed, preferred_element_type=jnp.float32)
    cache_ref[1] = x.astype(jnp.bfloat16)


def project(normed, wqkv, cosine, sine, parts):
    width, rows = normed.shape
    pairs = width // PAIR
    table = pl.BlockSpec((HD, rows), lambda i: (0, 0))
    query = len(parts) == 1

    def weight(j):
        return pl.BlockSpec((1, 2 * PAIR, width), lambda i: (j, i, 0))

    if query:
        out_spec = pl.BlockSpec((2, PAIR, rows), lambda i: (i, 0, 0))
        out_shape = jax.ShapeDtypeStruct((pairs, PAIR, rows), jnp.bfloat16)
    else:
        out_spec = pl.BlockSpec((2, 2 * PAIR, rows), lambda i: (0, i, 0))
        out_shape = jax.ShapeDtypeStruct((2, width, rows), jnp.bfloat16)
    return pl.pallas_call(
        query_body if query else cache_body,
        grid=(pairs // 2,),
        in_specs=[pl.BlockSpec((width, rows), lambda i: (0, 0))]
        + [weight(j) for j in parts]
        + [table, table],
        out_specs=out_spec,
        out_shape=out_shape,
        compiler_params=pltpu.CompilerParams(vmem_limit_bytes=VMEM),
        cost_estimate=pl.CostEstimate(
            flops=2 * len(parts) * width * width * rows,
            bytes_accessed=3 * len(parts) * width * width,
            transcendentals=0,
        ),
        name="project_query" if query else "project_cache",
    )(normed, *([wqkv] * len(parts)), cosine, sine)


def split_three(x):
    high = x.astype(jnp.bfloat16).astype(jnp.float32)
    middle = (x - high).astype(jnp.bfloat16).astype(jnp.float32)
    return high, middle, x - high - middle


def attend_pair(query, keys, values, old, own, out):
    rows = query.shape[1]
    step = min(256, rows)
    extra = jnp.where(lax.broadcasted_iota(jnp.int32, (EXT - PAIR, rows), 0) == 0, 1.0, 0.0)
    turned = jnp.transpose(jnp.concatenate([query, extra.astype(jnp.bfloat16)], axis=0))
    column = lax.broadcasted_iota(jnp.int32, (step, EXT), 1)
    ahead = lax.broadcasted_iota(jnp.int32, (step, step), 1) > lax.broadcasted_iota(jnp.int32, (step, step), 0)
    factor = math.log2(math.e) * HD ** (-0.5)
    for first in range(0, rows, step):
        count = old + (first + step if own else 0)
        parts = []
        for h in range(2):
            used = (column // HD == h) | (column == PAIR)
            mine = jnp.where(used, turned[first : first + step], 0).astype(jnp.bfloat16)
            scores = jnp.dot(mine, keys[:, :count], preferred_element_type=jnp.float32)
            if own:
                last = jnp.where(ahead, MASKED, scores[:, count - step :])
                scores = jnp.concatenate([scores[:, : count - step], last], axis=1)
            highest = jnp.max(scores, axis=1, keepdims=True)
            expo = jnp.exp2((scores - highest) * factor).astype(jnp.bfloat16)
            mixed = lax.dot_general(
                expo, values[:, :count], (((1,), (1,)), ((), ())), preferred_element_type=jnp.float32
            )
            total = mixed[:, PAIR : PAIR + 1]
            parts.append((mixed / total, split_three(highest * factor + jnp.log2(total))))
        result = jnp.where(column < HD, parts[0][0], parts[1][0])
        for h in range(2):
            for j in range(3):
                result = jnp.where(column == PAIR + 2 * j + h, parts[h][1][j], result)
        result = jnp.where(column >= PAIR + 6, 0.0, result)
        out[:, first : first + step] = jnp.transpose(result).astype(jnp.bfloat16)


def attend_body(arrived_ref, bias_ref, query_ref, own_ref, out_ref, kv, *, own_rows):
    old = bias_ref.shape[1]
    lower = lax.broadcasted_iota(jnp.int32, (EXT - PAIR, old + own_rows), 0)
    masks = jnp.concatenate([bias_ref[...], jnp.zeros((1, own_rows), jnp.float32)], axis=1)
    for g in range(2):
        kv[g, PAIR:EXT] = jnp.where(lower == 0, masks, 0.0).astype(jnp.bfloat16)
        kv[2 + g, PAIR:EXT] = jnp.where(lower == 0, 1.0, 0.0).astype(jnp.bfloat16)
        kv[g, 0:PAIR, old:] = own_ref[0, g * PAIR : (g + 1) * PAIR]
        kv[2 + g, 0:PAIR, old:] = own_ref[1, g * PAIR : (g + 1) * PAIR]
    for t in range(old // LANES):
        tiles = [arrived_ref[4 * t + j, 0] for j in range(4)]
        for g in range(4):
            kv[g, 0:PAIR, t * LANES : (t + 1) * LANES] = jnp.concatenate(
                [tile[:, g * BS : (g + 1) * BS] for tile in tiles], axis=1
            )
    for g in range(2):
        attend_pair(query_ref[g], kv.at[g], kv.at[2 + g], old, True, out_ref.at[g])


def attend_unit(arrived, place, bias, queries, new_cache, unit):
    rows = queries.shape[2]
    old = bias.shape[1]
    work = 4 * rows * (old + rows)
    return pl.pallas_call(
        functools.partial(attend_body, own_rows=rows),
        grid=(1,),
        in_specs=[
            pl.BlockSpec((arrived.shape[0], 1, PAIR, LANES), lambda i: (0, place, 0, 0)),
            pl.BlockSpec((1, old), lambda i: (0, 0)),
            pl.BlockSpec((2, PAIR, rows), lambda i: (unit, 0, 0)),
            pl.BlockSpec((2, 2 * PAIR, rows), lambda i: (0, unit, 0)),
        ],
        out_specs=pl.BlockSpec((2, EXT, rows), lambda i: (0, 0, 0)),
        out_shape=jax.ShapeDtypeStruct((2, EXT, rows), jnp.bfloat16),
        scratch_shapes=[pltpu.VMEM((4, EXT, old + rows), jnp.bfloat16)],
        compiler_params=pltpu.CompilerParams(vmem_limit_bytes=VMEM // 2),
        cost_estimate=pl.CostEstimate(
            flops=work * 1024, bytes_accessed=4000000, transcendentals=work
        ),
        name="attend_heads",
    )(arrived, bias, queries, new_cache)


def star_body(*refs, sources):
    query_ref, out_ref, kv = refs[sources:]
    lower = lax.broadcasted_iota(jnp.int32, (EXT - PAIR, sources * LANES), 0)
    kv[0, PAIR:EXT] = jnp.zeros(lower.shape, jnp.bfloat16)
    kv[1, PAIR:EXT] = jnp.where(lower == 0, 1.0, 0.0).astype(jnp.bfloat16)
    for s in range(sources):
        for c in range(2):
            kv[c, 0:PAIR, s * LANES : (s + 1) * LANES] = refs[s][0, c]
    attend_pair(query_ref[0], kv.at[0], kv.at[1], sources * LANES, False, out_ref)


def star_attend(arrived, query):
    sources = len(arrived)
    rows = query.shape[2]
    work = 2 * rows * sources * LANES
    return pl.pallas_call(
        functools.partial(star_body, sources=sources),
        out_shape=jax.ShapeDtypeStruct((EXT, rows), jnp.bfloat16),
        scratch_shapes=[pltpu.VMEM((2, EXT, sources * LANES), jnp.bfloat16)],
        compiler_params=pltpu.CompilerParams(vmem_limit_bytes=VMEM),
        cost_estimate=pl.CostEstimate(
            flops=work * 1024, bytes_accessed=1500000, transcendentals=work
        ),
        name="attend_longest",
    )(*arrived, query)


def fold_two(first, second):
    def logs(x):
        return [x[PAIR + h : PAIR + h + 1] + x[PAIR + 2 + h : PAIR + 3 + h] + x[PAIR + 4 + h : PAIR + 5 + h] for h in range(2)]

    logs_a, logs_b = logs(first), logs(second)
    heads, below = [], []
    for h in range(2):
        top = jnp.maximum(logs_a[h], logs_b[h])
        share_a, share_b = jnp.exp2(logs_a[h] - top), jnp.exp2(logs_b[h] - top)
        total = share_a + share_b
        span = slice(h * HD, (h + 1) * HD)
        heads.append((first[span] * share_a + second[span] * share_b) / total)
        below.append(split_three(top + jnp.log2(total)))
    return heads, below


def fold_body(first_ref, second_ref, out_ref):
    heads, below = fold_two(first_ref[...].astype(jnp.float32), second_ref[...].astype(jnp.float32))
    row = lax.broadcasted_iota(jnp.int32, (EXT - PAIR, out_ref.shape[1]), 0)
    lower = jnp.zeros(row.shape, jnp.float32)
    for j in range(3):
        for h in range(2):
            lower = jnp.where(row == 2 * j + h, below[h][j], lower)
    out_ref[...] = jnp.concatenate(heads + [lower], axis=0).astype(jnp.bfloat16)


def fold(first, second):
    return pl.pallas_call(
        fold_body,
        out_shape=jax.ShapeDtypeStruct(first.shape, jnp.bfloat16),
        compiler_params=pltpu.CompilerParams(vmem_limit_bytes=VMEM),
        name="fold_parts",
    )(first, second)


def finish_body(scalars, own_ref, other_ref, *refs):
    units, out_ref, held = refs[:-2], refs[-2], refs[-1]
    pairs = held.shape[0]
    for i in range(pairs):
        out_ref[i * PAIR : (i + 1) * PAIR] = units[i // 2][i % 2, 0:PAIR]

    @pl.when(scalars[0] == 1)
    def _():
        for i in range(pairs):
            held[i] = units[i // 2][i % 2]
        for i in range(pairs):
            pair = scalars[1] ^ i
            star = own_ref[i] if i < pairs // 2 else other_ref[i - pairs // 2]
            heads, _ = fold_two(held[pair].astype(jnp.float32), star.astype(jnp.float32))
            span = pl.ds(pl.multiple_of(pair * PAIR, 16), PAIR)
            out_ref[span] = jnp.concatenate(heads, axis=0).astype(jnp.bfloat16)


def finish(scalars, own, other, units):
    pairs = 2 * own.shape[0]
    rows = own.shape[2]
    return pl.pallas_call(
        finish_body,
        grid_spec=pltpu.PrefetchScalarGridSpec(
            num_scalar_prefetch=1,
            grid=(1,),
            in_specs=[pl.BlockSpec(x.shape, lambda i, s: (0, 0, 0)) for x in [own, other] + units],
            out_specs=pl.BlockSpec((pairs * PAIR, rows), lambda i, s: (0, 0)),
            scratch_shapes=[pltpu.VMEM((pairs, EXT, rows), jnp.bfloat16)],
        ),
        out_shape=jax.ShapeDtypeStruct((pairs * PAIR, rows), jnp.bfloat16),
        compiler_params=pltpu.CompilerParams(vmem_limit_bytes=VMEM),
        name="finish_heads",
    )(scalars, own, other, *units)


def merge_body(slots, vision_ref, gain_ref, weight_ref, out_ref, total, *, rows_here, width):
    step = pl.program_id(0)
    floats = vision_ref[0].astype(jnp.float32)
    average = jnp.sum(floats, axis=1, keepdims=True) / D
    spread = jnp.sum(floats * floats, axis=1, keepdims=True) / D - average * average
    normed = ((floats - average) * lax.rsqrt(spread + 1e-06) * gain_ref[...]).astype(jnp.bfloat16)
    product = jnp.dot(normed, weight_ref[0], preferred_element_type=jnp.float32)

    @pl.when(step == 0)
    def _():
        total[...] = product

    @pl.when(step > 0)
    def _():
        total[...] += product

    @pl.when(step == pl.num_programs(0) - 1)
    def _():
        devices, piece_rows = out_ref.shape[:2]
        groups = total.shape[0]
        pieces = groups // piece_rows
        shape = (devices * piece_rows, groups)
        row = lax.broadcasted_iota(jnp.int32, shape, 0)
        column = lax.broadcasted_iota(jnp.int32, shape, 1)
        label_row = lax.broadcasted_iota(jnp.int32, (groups, LANES), 0) // piece_rows
        target = jnp.zeros(shape, jnp.int32)
        label = jnp.zeros(label_row.shape, jnp.float32)
        for j in range(pieces):
            target = jnp.where(column // piece_rows == j, slots[j] // rows_here, target)
            place = (slots[j] % rows_here // piece_rows + 1).astype(jnp.float32)
            label = jnp.where(label_row == j, place, label)
        hit = (target == row // piece_rows) & (column % piece_rows == row % piece_rows)
        select = jnp.where(hit, 1.0, 0.0).astype(jnp.bfloat16)
        wide = jnp.concatenate([total[...].astype(jnp.bfloat16), label.astype(jnp.bfloat16)], axis=1)
        sent = jnp.dot(select, wide, preferred_element_type=jnp.float32).astype(jnp.bfloat16)
        for w in range(devices):
            out_ref[w] = sent[w * piece_rows : (w + 1) * piece_rows]


def merge_rows(vision, ln_gain, merge_proj, image_slot, rows_here):
    parts, width, groups = vision.shape
    devices = lax.axis_size("blk")
    piece_rows = groups // image_slot.shape[0]
    return pl.pallas_call(
        functools.partial(merge_body, rows_here=rows_here, width=width),
        grid_spec=pltpu.PrefetchScalarGridSpec(
            num_scalar_prefetch=1,
            grid=(parts,),
            in_specs=[
                pl.BlockSpec((1, groups, width), lambda i, s: (i, 0, 0)),
                pl.BlockSpec((1, width), lambda i, s: (0, 0)),
                pl.BlockSpec((1, width, width), lambda i, s: (i, 0, 0)),
            ],
            out_specs=pl.BlockSpec((devices, piece_rows, width + LANES), lambda i, s: (0, 0, 0)),
            scratch_shapes=[pltpu.VMEM((groups, width), jnp.float32)],
        ),
        out_shape=jax.ShapeDtypeStruct((devices, piece_rows, width + LANES), jnp.bfloat16),
        compiler_params=pltpu.CompilerParams(vmem_limit_bytes=VMEM),
        cost_estimate=pl.CostEstimate(
            flops=2 * groups * parts * width * width,
            bytes_accessed=2 * parts * width * width,
            transcendentals=0,
        ),
        name="merge_pieces",
    )(image_slot, jnp.transpose(vision, (0, 2, 1)), ln_gain.reshape(1, width), merge_proj)


def place_and_norm(arrived, text, rms_gain):
    width, rows_here = text.shape
    devices, piece_rows = arrived.shape[:2]
    lines = jnp.arange(rows_here, dtype=jnp.int32)
    offsets = jnp.arange(piece_rows, dtype=jnp.int32)
    starts = (arrived[:, 0, width].astype(jnp.int32) - 1) * piece_rows
    row_ids = (starts[:, None] + offsets[None, :]).reshape(-1)
    present = jnp.repeat(starts >= 0, piece_rows)
    hits = (row_ids[:, None] == lines[None, :]) & present[:, None]
    placed_rows = jnp.einsum(
        "kl,kr->lr",
        arrived[:, :, :width].reshape(devices * piece_rows, width),
        hits.astype(jnp.bfloat16),
        preferred_element_type=jnp.float32,
    ).astype(jnp.bfloat16)
    covered = jnp.any(hits, axis=0)
    placed = jnp.where(covered[None, :], placed_rows, text)
    row_floats = placed.astype(jnp.float32)
    square_sums = jnp.sum(row_floats * row_floats, axis=0)
    return (row_floats * lax.rsqrt(square_sums / D + 1e-06)[None, :] * rms_gain[:, None]).astype(
        jnp.bfloat16
    )


def rotary_tables(places):
    half = HD // 2
    freq_index = jnp.arange(half, dtype=jnp.float32)
    inverse = jnp.exp(freq_index * (-2.0 * math.log(10000.0) / HD))
    angles = inverse[:, None] * places[None, :]
    cosine = jnp.cos(angles)
    sine = jnp.sin(angles)
    return jnp.concatenate([cosine, cosine], axis=0), jnp.concatenate([-sine, sine], axis=0)


def swap(x, bit):
    size = lax.axis_size("blk")
    return lax.ppermute(x, "blk", [(i, i ^ (1 << bit)) for i in range(size)])


def spread_shards(
    vision, ln_gain, merge_proj, image_slot, text, rms_gain, wqkv, pcache, block_table, cache_len
):
    devices = lax.axis_size("blk")
    here = lax.axis_index("blk")
    width, rows = text.shape
    pairs = width // PAIR
    owned = pcache.shape[2] // BS
    table_width = block_table.shape[1]
    each = table_width // devices

    tie = lax.optimization_barrier
    outbound = merge_rows(vision, ln_gain, merge_proj, image_slot, rows)
    outbound, block_table = tie((outbound, block_table))
    holder = jnp.where(block_table >= 0, block_table // owned, -1)
    local = block_table - here * owned
    mine = holder == here
    longest = jnp.argmax(block_table[:, table_width - 1]).astype(jnp.int32)
    chosen = jnp.max(jnp.where(mine, local, 0), axis=1)
    star_row = jnp.where(
        lax.dynamic_index_in_dim(mine, longest, 0, False),
        lax.dynamic_index_in_dim(local, longest, 0, False),
        -1,
    )
    rank = jnp.sum((star_row[None, :] > star_row[:, None]).astype(jnp.int32), axis=1)
    star_ids = jnp.sum(
        jnp.where(
            (rank[None, :] == jnp.arange(each, dtype=jnp.int32)[:, None]) & (star_row >= 0)[None, :],
            star_row[None, :],
            0,
        ),
        axis=1,
    )
    row_holder = lax.dynamic_index_in_dim(holder, here, 0, False)
    row_count = jnp.clip(cache_len[0] - BS * jnp.arange(table_width, dtype=jnp.int32), 0, BS)
    live = jnp.sum(
        jnp.where(
            row_holder[None, :] == jnp.arange(devices, dtype=jnp.int32)[:, None], row_count[None, :], 0
        ),
        axis=1,
    )
    live = jnp.where(here == longest, 0, live)
    bias = jnp.where(jnp.arange(BS, dtype=jnp.int32)[None, :] < live[:, None], 0.0, MASKED)
    bias = bias.astype(jnp.float32).reshape(1, devices * BS)

    paged = pcache.reshape(2, pairs, PAIR, owned * BS)
    units = pairs // 2

    def exchange(x):
        return lax.all_to_all(x, "blk", split_axis=0, concat_axis=0, tiled=True)

    pieces_in = exchange(outbound)
    head = units - 1
    packed = pack_units(chosen, paged, 0, head)
    packed, pieces_in = tie((packed, pieces_in))
    arrived = exchange(packed)
    packed_last = pack_units(chosen, paged, head, units - head)

    normed = place_and_norm(pieces_in, text, rms_gain)
    normed, packed_last = tie((normed, packed_last))
    places = (cache_len[0] + jnp.arange(rows, dtype=jnp.int32)).astype(jnp.float32)
    tables = rotary_tables(places)
    queries = project(normed, wqkv, *tables, (0,))

    plane_bits = pairs.bit_length() - 1
    all_bits = devices.bit_length() - 1
    place = here % pairs
    pair = place % 2 * 4 + place // 2 % 2 * 2 + place // 4
    query = queries
    for bit in range(plane_bits):
        mine_bit, star_bit = (here >> bit) & 1, (longest >> bit) & 1
        halves = query.reshape(2, query.shape[0] // 2, PAIR, rows)
        kept = lax.dynamic_index_in_dim(halves, mine_bit, 0, False)
        given = lax.dynamic_index_in_dim(halves, 1 - mine_bit, 0, False)
        taken = swap(given, bit)
        if bit == 0:
            normed, taken = tie((normed, taken))
            new_cache = project(normed, wqkv, *tables, (1, 2))
        if bit == 1:
            taken, new_cache = tie((taken, new_cache))
            star_ids, taken = tie((star_ids, taken))
            star_ids = jnp.concatenate([pair.astype(jnp.int32).reshape(1), star_ids])
            star_kv = star_pack(star_ids, paged)
        if bit == 2:
            taken, star_kv = tie((taken, star_kv))
            star_parts = [star_kv[0:1]]
            for i in range(1, pairs):
                away = i % 2 * 4 + i // 2 % 2 * 2 + i // 4
                star_parts.append(
                    lax.ppermute(star_kv[i : i + 1], "blk", [(d, d ^ away) for d in range(devices)])
                )
        query = jnp.where(star_bit == mine_bit, kept, taken)
    for bit in range(plane_bits, all_bits):
        same = ((here ^ longest) >> bit) & 1
        query = jnp.where(same == 0, query, swap(query, bit))
    star_parts, query = tie((star_parts, query))
    star = star_attend(star_parts, query)
    results = []
    came = [arrived]

    def attend_next(*after):
        u = len(results)
        held, *_ = tie((bias, *after))
        chunk, place = (came[0], u) if u < head else (came[1], u - head)
        results.append(attend_unit(chunk, place, held, queries, new_cache, u))

    half = pairs // 2
    mates = [i % 2 * 4 + i // 2 % 2 * 2 + i // 4 for i in range(half)]
    for bit in range(plane_bits, all_bits):
        other = swap(star, bit)
        if bit == all_bits - 1:
            attend_next(star)
            other, results = tie((other, results))
            packed_last, came[0], other = tie((packed_last, came[0], other))
            came.append(exchange(packed_last))
        star = fold(star, other)
    own = [star]
    for away in mates[1:]:
        own.append(lax.ppermute(star, "blk", [(d, d ^ away) for d in range(devices)]))
    while len(results) < head:
        attend_next(star)
    own, results = tie((own, results))
    own = jnp.stack(own)
    other = swap(own, 0)
    while len(results) < units:
        attend_next(own)
    other, results = tie((other, results))
    scalars = jnp.stack([(here == longest).astype(jnp.int32), pair.astype(jnp.int32)])
    return (finish(scalars, own, other, results), new_cache)


def spreads(mesh):
    devices = mesh.shape["blk"]
    pairs = D // PAIR
    return mesh.shape["head"] == 1 and devices % pairs == 0 and devices & (devices - 1) == 0


def solution(mesh):
    in_specs = (
        P(None, "head", "blk"),
        P("head"),
        P(None, "head", None),
        P("blk"),
        P("head", "blk"),
        P(),
        P(None, "head", None),
        P(None, "head", "blk"),
        P(),
        P("blk"),
    )
    out_specs = (P("head", "blk"), P(None, "head", "blk"))
    body = spread_shards if spreads(mesh) else shards
    return jax.shard_map(body, mesh=mesh, in_specs=in_specs, out_specs=out_specs, check_vma=False)
```

```python
import functools
import math

import jax
import jax.numpy as jnp
from jax import lax
from jax.experimental import pallas as pl
from jax.experimental.pallas import tpu as pltpu
from jax.sharding import PartitionSpec as P

D = 1408
HD = 88
BS = 32
PAIR = 2 * HD
EXT = PAIR + 16
LANES = 128
MASKED = -1e30
VMEM = 60 * 1024 * 1024


masked_score = -1e30


def rotary_columns(values, places):
    half = values.shape[1] // 2
    freq_index = jnp.arange(half, dtype=jnp.float32)
    inverse = jnp.exp(freq_index * (-2.0 * math.log(10000.0) / values.shape[1]))
    angles = inverse[:, None] * places[None, :]
    cosine = jnp.cos(angles)[None]
    sine_part = jnp.sin(angles)[None]
    leading = values[:, :half]
    trailing = values[:, half:]
    return jnp.concatenate(
        [leading * cosine - trailing * sine_part, trailing * cosine + leading * sine_part], axis=1
    )


def softmax_part(query_block, keys, values, mask, scale):
    scores = (
        jnp.einsum("hdq,hdk->hqk", query_block, keys, preferred_element_type=jnp.float32) * scale
    )
    scores = jnp.where(mask[None], scores, masked_score)
    highest = jnp.max(scores, axis=2)
    expo = jnp.where(mask[None], jnp.exp(scores - highest[:, :, None]), 0.0)
    total = jnp.sum(expo, axis=2)
    mixed = jnp.einsum("hqk,hdk->hdq", expo, values, precision=lax.Precision.HIGHEST)
    return (mixed, highest, total)


def fold_softmax(first, second):
    mixed_a, high_a, total_a = first
    mixed_b, high_b, total_b = second
    top = jnp.maximum(high_a, high_b)
    factor_a = jnp.exp(high_a - top)
    factor_b = jnp.exp(high_b - top)
    return (
        mixed_a * factor_a[:, None, :] + mixed_b * factor_b[:, None, :],
        top,
        total_a * factor_a + total_b * factor_b,
    )


def unblock(parts):
    mixed, highest, total = parts
    heads_here = mixed.shape[1]
    mixed = jnp.transpose(mixed, (1, 2, 0, 3)).reshape(heads_here, mixed.shape[2], -1)
    highest = jnp.transpose(highest, (1, 0, 2)).reshape(heads_here, -1)
    total = jnp.transpose(total, (1, 0, 2)).reshape(heads_here, -1)
    return (mixed, highest, total)


def shards(
    vision, ln_gain, merge_proj, image_slot, text, rms_gain, wqkv, pcache, block_table, cache_len
):
    local = vision.shape[1]
    groups = vision.shape[2]
    floats = vision.astype(jnp.float32)
    totals, squares = lax.psum((jnp.sum(floats, axis=1), jnp.sum(floats * floats, axis=1)), "head")
    average = totals / D
    spread = squares / D - average * average
    normed_vision = (
        (floats - average[:, None, :])
        * lax.rsqrt(spread + 1e-06)[:, None, :]
        * ln_gain[None, :, None]
    ).astype(jnp.bfloat16)
    partial_rows = jnp.einsum(
        "tcd,tcg->dg", merge_proj, normed_vision, preferred_element_type=jnp.float32
    )
    merged_columns = lax.psum_scatter(partial_rows, "head", scatter_dimension=0, tiled=True).astype(
        jnp.bfloat16
    )
    merged = jnp.transpose(merged_columns)
    devices = lax.axis_size("blk")
    here = lax.axis_index("blk")
    rows_here = text.shape[1]
    pieces = image_slot.shape[0]
    piece_rows = groups // pieces
    lines = jnp.arange(rows_here, dtype=jnp.int32)
    offsets = jnp.arange(piece_rows, dtype=jnp.int32)
    target = image_slot // rows_here
    within = image_slot % rows_here
    select = target[None, :] == jnp.arange(devices, dtype=jnp.int32)[:, None]
    outbound = (
        jnp.dot(
            select.astype(jnp.bfloat16),
            merged.reshape(pieces, piece_rows * local),
            preferred_element_type=jnp.float32,
        )
        .astype(jnp.bfloat16)
        .reshape(devices, piece_rows, local)
    )
    starts = jnp.sum(jnp.where(select, within[None, :] + 1, 0), axis=1) - 1
    arrived, arrived_start = (
        lax.all_to_all(outbound, "blk", split_axis=0, concat_axis=0, tiled=True),
        lax.all_to_all(starts, "blk", split_axis=0, concat_axis=0, tiled=True),
    )
    row_ids = (arrived_start[:, None] + offsets[None, :]).reshape(-1)
    present = jnp.repeat(arrived_start >= 0, piece_rows)
    hits = (row_ids[:, None] == lines[None, :]) & present[:, None]
    placed_rows = jnp.einsum(
        "kl,kr->lr",
        arrived.reshape(devices * piece_rows, local),
        hits.astype(jnp.bfloat16),
        preferred_element_type=jnp.float32,
    ).astype(jnp.bfloat16)
    covered = jnp.any(hits, axis=0)
    placed = jnp.where(covered[None, :], placed_rows, text)
    row_floats = placed.astype(jnp.float32)
    square_sums = lax.psum(jnp.sum(row_floats * row_floats, axis=0), "head")
    gain_here = lax.dynamic_slice_in_dim(rms_gain, lax.axis_index("head") * local, local)
    normed = (row_floats * lax.rsqrt(square_sums / D + 1e-06)[None, :] * gain_here[:, None]).astype(
        jnp.bfloat16
    )
    projected = jnp.einsum(
        "jod,dr->jor",
        wqkv,
        lax.all_gather(normed, "head", axis=0, tiled=True),
        preferred_element_type=jnp.float32,
    )
    heads_here = local // HD
    projected = projected.reshape(3, heads_here, HD, rows_here)
    places = (cache_len[0] + lines).astype(jnp.float32)
    queries = rotary_columns(projected[0], places).astype(jnp.bfloat16)
    new_keys = rotary_columns(projected[1], places).astype(jnp.bfloat16)
    new_values = projected[2].astype(jnp.bfloat16)
    new_cache = jnp.stack(
        [new_keys.reshape(local, rows_here), new_values.reshape(local, rows_here)], axis=0
    )
    block_len = BS
    owned = pcache.shape[2] // block_len
    paged = pcache.reshape(2, local, owned, block_len)
    requests = block_table.shape[0]
    table_width = block_table.shape[1]
    slots_each = table_width // devices
    block_ids = here * owned + jnp.arange(owned, dtype=jnp.int32)
    matches = block_table[None, :, :] == block_ids[:, None, None]
    found = jnp.any(matches, axis=2)
    in_use = jnp.any(found, axis=1)
    owner = jnp.sum(jnp.where(found, jnp.arange(requests, dtype=jnp.int32)[None, :], 0), axis=1)
    logical = jnp.sum(
        jnp.where(matches, jnp.arange(table_width, dtype=jnp.int32)[None, None, :], 0), axis=(1, 2)
    )
    counter = jnp.arange(owned, dtype=jnp.int32)
    earlier = (
        (owner[:, None] == owner[None, :]) & in_use[None, :] & (counter[None, :] < counter[:, None])
    )
    standing = jnp.sum(earlier.astype(jnp.int32), axis=1)
    within_block = jnp.arange(block_len, dtype=jnp.int32)
    block_rows = min(rows_here, 512)
    count_blocks = rows_here // block_rows
    scale = HD ** (-0.5)
    query_blocks = jnp.transpose(
        queries.reshape(heads_here, HD, count_blocks, block_rows), (2, 0, 1, 3)
    )
    first_rows = jnp.arange(count_blocks, dtype=jnp.int32) * block_rows
    destination = owner * slots_each + standing
    routing = (destination[None, :] == jnp.arange(table_width, dtype=jnp.int32)[:, None]) & in_use[
        None, :
    ]
    outgoing = jnp.einsum(
        "wo,cfob->cfwb", routing.astype(jnp.bfloat16), paged, preferred_element_type=jnp.float32
    ).astype(jnp.bfloat16)
    outgoing = outgoing.reshape(2, local, table_width * block_len)
    labels = jnp.sum(jnp.where(routing, logical[None, :] + 1, 0), axis=1) - 1
    labels = labels.reshape(1, 1, table_width)
    blocks_in, labels_in = (
        lax.all_to_all(outgoing, "blk", split_axis=2, concat_axis=2, tiled=True),
        lax.all_to_all(labels, "blk", split_axis=2, concat_axis=2, tiled=True),
    )
    cached_keys = blocks_in[0].reshape(heads_here, HD, -1)
    cached_values = blocks_in[1].reshape(heads_here, HD, -1).astype(jnp.float32)
    label_flat = labels_in.reshape(-1)
    key_places = label_flat[:, None] * block_len + within_block[None, :]
    live = ((label_flat[:, None] >= 0) & (key_places < cache_len[0])).reshape(-1)
    old_mask = jnp.broadcast_to(live[None, :], (block_rows, live.shape[0]))
    new_values_f = new_values.astype(jnp.float32)

    def attend(inputs):
        query_block, first_row = inputs
        causal = (first_row + jnp.arange(block_rows, dtype=jnp.int32))[:, None] >= lines[None, :]
        old_part = softmax_part(query_block, cached_keys, cached_values, old_mask, scale)
        own_part = softmax_part(query_block, new_keys, new_values_f, causal, scale)
        return fold_softmax(old_part, own_part)

    mixed, highest, total = unblock(lax.map(attend, (query_blocks, first_rows)))
    attended = (mixed / total[:, None, :]).astype(jnp.bfloat16).reshape(local, rows_here)
    return (attended, new_cache)


def pack_body(ids, cache_ref, out_ref, *, slots):
    lane = lax.broadcasted_iota(jnp.int32, (PAIR, LANES), 1) // BS

    def one(w, carry):
        block = ids[w]
        start = pl.multiple_of(block // 4 * LANES, LANES)
        turn = block % 4
        packed = None
        for g in range(4):
            tile = cache_ref[g // 2, g % 2, :, pl.ds(start, LANES)]
            tile = pltpu.roll(tile, (g + 4 - turn) % 4 * BS, 1)
            packed = tile if g == 0 else jnp.where(lane == g, tile, packed)
        out_ref[w, 0] = packed
        return carry

    lax.fori_loop(0, slots, one, 0, unroll=8)


def pack_units(ids, paged, first, count):
    slots = ids.shape[0]
    lanes = paged.shape[3]
    return pl.pallas_call(
        functools.partial(pack_body, slots=slots),
        grid_spec=pltpu.PrefetchScalarGridSpec(
            num_scalar_prefetch=1,
            grid=(count,),
            in_specs=[pl.BlockSpec((2, 2, PAIR, lanes), lambda i, s: (0, first + i, 0, 0))],
            out_specs=pl.BlockSpec((slots, 1, PAIR, LANES), lambda i, s: (0, i, 0, 0)),
        ),
        out_shape=jax.ShapeDtypeStruct((slots, count, PAIR, LANES), jnp.bfloat16),
        compiler_params=pltpu.CompilerParams(vmem_limit_bytes=VMEM),
        cost_estimate=pl.CostEstimate(
            flops=0, bytes_accessed=4500000 * count, transcendentals=0
        ),
        name="pack_blocks",
    )(ids, paged)


def star_pack_body(ids, *refs):
    lane = lax.broadcasted_iota(jnp.int32, (PAIR, LANES), 1) // BS
    for c in range(2):
        packed = None
        for j in range(4):
            tile = pltpu.roll(refs[c * 4 + j][0, 0], (j + 4 - ids[1 + j] % 4) % 4 * BS, 1)
            packed = tile if j == 0 else jnp.where(lane == j, tile, packed)
        refs[8][0, c] = packed


def star_pack(ids, paged):
    pairs = paged.shape[1]

    def spec(c, j):
        return pl.BlockSpec((1, 1, PAIR, LANES), lambda i, s: (c, i ^ s[0], 0, s[1 + j] // 4))

    return pl.pallas_call(
        star_pack_body,
        grid_spec=pltpu.PrefetchScalarGridSpec(
            num_scalar_prefetch=1,
            grid=(pairs,),
            in_specs=[spec(c, j) for c in range(2) for j in range(4)],
            out_specs=pl.BlockSpec((1, 2, PAIR, LANES), lambda i, s: (i, 0, 0, 0)),
        ),
        out_shape=jax.ShapeDtypeStruct((pairs, 2, PAIR, LANES), jnp.bfloat16),
        compiler_params=pltpu.CompilerParams(vmem_limit_bytes=VMEM),
        cost_estimate=pl.CostEstimate(flops=0, bytes_accessed=4000000, transcendentals=0),
        name="pack_longest",
    )(ids, *([paged] * 8))


def rotate_heads(x, cosine, sine):
    heads = []
    for h in range(2):
        one = x[h * HD : (h + 1) * HD]
        other = jnp.concatenate([one[HD // 2 :], one[: HD // 2]], axis=0)
        heads.append(one * cosine + other * sine)
    return jnp.concatenate(heads, axis=0).astype(jnp.bfloat16)


def query_body(normed_ref, weight_ref, cos_ref, sin_ref, query_ref):
    x = jnp.dot(weight_ref[0], normed_ref[...], preferred_element_type=jnp.float32)
    for g in range(query_ref.shape[0]):
        query_ref[g] = rotate_heads(x[g * PAIR : (g + 1) * PAIR], cos_ref[...], sin_ref[...])


def cache_body(normed_ref, key_ref, value_ref, cos_ref, sin_ref, cache_ref):
    normed = normed_ref[...]
    x = jnp.dot(key_ref[0], normed, preferred_element_type=jnp.float32)
    for g in range(x.shape[0] // PAIR):
        span = slice(g * PAIR, (g + 1) * PAIR)
        cache_ref[0, span] = rotate_heads(x[span], cos_ref[...], sin_ref[...])
    x = jnp.dot(value_ref[0], normed, preferred_element_type=jnp.float32)
    cache_ref[1] = x.astype(jnp.bfloat16)


def project(normed, wqkv, cosine, sine, parts):
    width, rows = normed.shape
    pairs = width // PAIR
    table = pl.BlockSpec((HD, rows), lambda i: (0, 0))
    query = len(parts) == 1

    def weight(j):
        return pl.BlockSpec((1, 2 * PAIR, width), lambda i: (j, i, 0))

    if query:
        out_spec = pl.BlockSpec((2, PAIR, rows), lambda i: (i, 0, 0))
        out_shape = jax.ShapeDtypeStruct((pairs, PAIR, rows), jnp.bfloat16)
    else:
        out_spec = pl.BlockSpec((2, 2 * PAIR, rows), lambda i: (0, i, 0))
        out_shape = jax.ShapeDtypeStruct((2, width, rows), jnp.bfloat16)
    return pl.pallas_call(
        query_body if query else cache_body,
        grid=(pairs // 2,),
        in_specs=[pl.BlockSpec((width, rows), lambda i: (0, 0))]
        + [weight(j) for j in parts]
        + [table, table],
        out_specs=out_spec,
        out_shape=out_shape,
        compiler_params=pltpu.CompilerParams(vmem_limit_bytes=VMEM),
        cost_estimate=pl.CostEstimate(
            flops=2 * len(parts) * width * width * rows,
            bytes_accessed=3 * len(parts) * width * width,
            transcendentals=0,
        ),
        name="project_query" if query else "project_cache",
    )(normed, *([wqkv] * len(parts)), cosine, sine)


def split_three(x):
    high = x.astype(jnp.bfloat16).astype(jnp.float32)
    middle = (x - high).astype(jnp.bfloat16).astype(jnp.float32)
    return high, middle, x - high - middle


def attend_pair(query, keys, values, old, own, out):
    rows = query.shape[1]
    step = min(256, rows)
    extra = jnp.where(lax.broadcasted_iota(jnp.int32, (EXT - PAIR, rows), 0) == 0, 1.0, 0.0)
    turned = jnp.transpose(jnp.concatenate([query, extra.astype(jnp.bfloat16)], axis=0))
    column = lax.broadcasted_iota(jnp.int32, (step, EXT), 1)
    ahead = lax.broadcasted_iota(jnp.int32, (step, step), 1) > lax.broadcasted_iota(jnp.int32, (step, step), 0)
    factor = math.log2(math.e) * HD ** (-0.5)
    for first in range(0, rows, step):
        count = old + (first + step if own else 0)
        parts = []
        for h in range(2):
            used = (column // HD == h) | (column == PAIR)
            mine = jnp.where(used, turned[first : first + step], 0).astype(jnp.bfloat16)
            scores = jnp.dot(mine, keys[:, :count], preferred_element_type=jnp.float32)
            if own:
                last = jnp.where(ahead, MASKED, scores[:, count - step :])
                scores = jnp.concatenate([scores[:, : count - step], last], axis=1)
            highest = jnp.max(scores, axis=1, keepdims=True)
            expo = jnp.exp2((scores - highest) * factor).astype(jnp.bfloat16)
            mixed = lax.dot_general(
                expo, values[:, :count], (((1,), (1,)), ((), ())), preferred_element_type=jnp.float32
            )
            total = mixed[:, PAIR : PAIR + 1]
            parts.append((mixed / total, split_three(highest * factor + jnp.log2(total))))
        result = jnp.where(column < HD, parts[0][0], parts[1][0])
        for h in range(2):
            for j in range(3):
                result = jnp.where(column == PAIR + 2 * j + h, parts[h][1][j], result)
        result = jnp.where(column >= PAIR + 6, 0.0, result)
        out[:, first : first + step] = jnp.transpose(result).astype(jnp.bfloat16)


def attend_body(arrived_ref, bias_ref, query_ref, own_ref, out_ref, kv, *, own_rows):
    old = bias_ref.shape[1]
    lower = lax.broadcasted_iota(jnp.int32, (EXT - PAIR, old + own_rows), 0)
    masks = jnp.concatenate([bias_ref[...], jnp.zeros((1, own_rows), jnp.float32)], axis=1)
    for g in range(2):
        kv[g, PAIR:EXT] = jnp.where(lower == 0, masks, 0.0).astype(jnp.bfloat16)
        kv[2 + g, PAIR:EXT] = jnp.where(lower == 0, 1.0, 0.0).astype(jnp.bfloat16)
        kv[g, 0:PAIR, old:] = own_ref[0, g * PAIR : (g + 1) * PAIR]
        kv[2 + g, 0:PAIR, old:] = own_ref[1, g * PAIR : (g + 1) * PAIR]
    for t in range(old // LANES):
        tiles = [arrived_ref[4 * t + j, 0] for j in range(4)]
        for g in range(4):
            kv[g, 0:PAIR, t * LANES : (t + 1) * LANES] = jnp.concatenate(
                [tile[:, g * BS : (g + 1) * BS] for tile in tiles], axis=1
            )
    for g in range(2):
        attend_pair(query_ref[g], kv.at[g], kv.at[2 + g], old, True, out_ref.at[g])


def attend_unit(arrived, place, bias, queries, new_cache, unit):
    rows = queries.shape[2]
    old = bias.shape[1]
    work = 4 * rows * (old + rows)
    return pl.pallas_call(
        functools.partial(attend_body, own_rows=rows),
        grid=(1,),
        in_specs=[
            pl.BlockSpec((arrived.shape[0], 1, PAIR, LANES), lambda i: (0, place, 0, 0)),
            pl.BlockSpec((1, old), lambda i: (0, 0)),
            pl.BlockSpec((2, PAIR, rows), lambda i: (unit, 0, 0)),
            pl.BlockSpec((2, 2 * PAIR, rows), lambda i: (0, unit, 0)),
        ],
        out_specs=pl.BlockSpec((2, EXT, rows), lambda i: (0, 0, 0)),
        out_shape=jax.ShapeDtypeStruct((2, EXT, rows), jnp.bfloat16),
        scratch_shapes=[pltpu.VMEM((4, EXT, old + rows), jnp.bfloat16)],
        compiler_params=pltpu.CompilerParams(vmem_limit_bytes=VMEM),
        cost_estimate=pl.CostEstimate(
            flops=work * 1024, bytes_accessed=4000000, transcendentals=work
        ),
        name="attend_heads",
    )(arrived, bias, queries, new_cache)


def star_body(*refs, sources):
    query_ref, out_ref, kv = refs[sources:]
    lower = lax.broadcasted_iota(jnp.int32, (EXT - PAIR, sources * LANES), 0)
    kv[0, PAIR:EXT] = jnp.zeros(lower.shape, jnp.bfloat16)
    kv[1, PAIR:EXT] = jnp.where(lower == 0, 1.0, 0.0).astype(jnp.bfloat16)
    for s in range(sources):
        for c in range(2):
            kv[c, 0:PAIR, s * LANES : (s + 1) * LANES] = refs[s][0, c]
    attend_pair(query_ref[0], kv.at[0], kv.at[1], sources * LANES, False, out_ref)


def star_attend(arrived, query):
    sources = len(arrived)
    rows = query.shape[2]
    work = 2 * rows * sources * LANES
    return pl.pallas_call(
        functools.partial(star_body, sources=sources),
        out_shape=jax.ShapeDtypeStruct((EXT, rows), jnp.bfloat16),
        scratch_shapes=[pltpu.VMEM((2, EXT, sources * LANES), jnp.bfloat16)],
        compiler_params=pltpu.CompilerParams(vmem_limit_bytes=VMEM),
        cost_estimate=pl.CostEstimate(
            flops=work * 1024, bytes_accessed=1500000, transcendentals=work
        ),
        name="attend_longest",
    )(*arrived, query)


def fold_two(first, second):
    def logs(x):
        return [x[PAIR + h : PAIR + h + 1] + x[PAIR + 2 + h : PAIR + 3 + h] + x[PAIR + 4 + h : PAIR + 5 + h] for h in range(2)]

    logs_a, logs_b = logs(first), logs(second)
    heads, below = [], []
    for h in range(2):
        top = jnp.maximum(logs_a[h], logs_b[h])
        share_a, share_b = jnp.exp2(logs_a[h] - top), jnp.exp2(logs_b[h] - top)
        total = share_a + share_b
        span = slice(h * HD, (h + 1) * HD)
        heads.append((first[span] * share_a + second[span] * share_b) / total)
        below.append(split_three(top + jnp.log2(total)))
    return heads, below


def fold_body(first_ref, second_ref, out_ref):
    heads, below = fold_two(first_ref[...].astype(jnp.float32), second_ref[...].astype(jnp.float32))
    row = lax.broadcasted_iota(jnp.int32, (EXT - PAIR, out_ref.shape[1]), 0)
    lower = jnp.zeros(row.shape, jnp.float32)
    for j in range(3):
        for h in range(2):
            lower = jnp.where(row == 2 * j + h, below[h][j], lower)
    out_ref[...] = jnp.concatenate(heads + [lower], axis=0).astype(jnp.bfloat16)


def fold(first, second):
    return pl.pallas_call(
        fold_body,
        out_shape=jax.ShapeDtypeStruct(first.shape, jnp.bfloat16),
        compiler_params=pltpu.CompilerParams(vmem_limit_bytes=VMEM),
        name="fold_parts",
    )(first, second)


def finish_pairs(longest, stars, parts, out_ref):
    @pl.when(jnp.logical_not(longest))
    def _():
        for i, part in enumerate(parts):
            out_ref[i * PAIR : (i + 1) * PAIR] = part[0:PAIR]

    @pl.when(longest)
    def _():
        for i, part in enumerate(parts):
            heads, _ = fold_two(part[...].astype(jnp.float32), stars[i]().astype(jnp.float32))
            out_ref[i * PAIR : (i + 1) * PAIR] = jnp.concatenate(heads, axis=0).astype(jnp.bfloat16)


def finish_body(scalars, own_ref, other_ref, *refs):
    parts = [ref.at[g] for ref in refs[:-1] for g in range(2)]
    half = own_ref.shape[0]

    def star(i):
        place = scalars[1] ^ i
        return jnp.where(place < half, own_ref[place % half], other_ref[place % half])

    stars = [functools.partial(star, i) for i in range(len(parts))]
    finish_pairs(scalars[0] == 1, stars, parts, refs[-1])


def finish(scalars, own, other, units):
    half, _, rows = own.shape
    return pl.pallas_call(
        finish_body,
        grid_spec=pltpu.PrefetchScalarGridSpec(
            num_scalar_prefetch=1,
            grid=(1,),
            in_specs=[pl.BlockSpec(x.shape, lambda i, s: (0, 0, 0)) for x in [own, other] + units],
            out_specs=pl.BlockSpec((2 * len(units) * PAIR, rows), lambda i, s: (0, 0)),
        ),
        out_shape=jax.ShapeDtypeStruct((2 * half * PAIR, rows), jnp.bfloat16),
        compiler_params=pltpu.CompilerParams(vmem_limit_bytes=VMEM),
        name="finish_heads",
    )(scalars, own, other, *units)


def last_body(scalars, arrived, bias, query, cache, *refs, rows, unit, half):
    own, other, out_ref, kv, part = refs[0:2], refs[2:4], *refs[5:]
    attend_body(arrived, bias, query, cache, part, kv, own_rows=rows)

    def star(g):
        return jnp.where((scalars[1] ^ (2 * unit + g)) < half, own[g][0], other[g][0])

    stars = [functools.partial(star, g) for g in range(2)]
    finish_pairs(scalars[0] == 1, stars, [part.at[0], part.at[1]], out_ref)


def attend_last(scalars, arrived, bias, queries, new_cache, own, other, output, unit):
    rows = queries.shape[2]
    old = bias.shape[1]
    work = 4 * rows * (old + rows)
    half = own.shape[0]

    def star_spec(g):
        return pl.BlockSpec((1, EXT, rows), lambda i, s: ((s[1] ^ (2 * unit + g)) % half, 0, 0))

    return pl.pallas_call(
        functools.partial(last_body, rows=rows, unit=unit, half=half),
        grid_spec=pltpu.PrefetchScalarGridSpec(
            num_scalar_prefetch=1,
            grid=(1,),
            in_specs=[
                pl.BlockSpec((arrived.shape[0], 1, PAIR, LANES), lambda i, s: (0, 0, 0, 0)),
                pl.BlockSpec((1, old), lambda i, s: (0, 0)),
                pl.BlockSpec((2, PAIR, rows), lambda i, s: (unit, 0, 0)),
                pl.BlockSpec((2, 2 * PAIR, rows), lambda i, s: (0, unit, 0)),
                star_spec(0),
                star_spec(1),
                star_spec(0),
                star_spec(1),
                pl.BlockSpec(memory_space=pl.ANY),
            ],
            out_specs=pl.BlockSpec((2 * PAIR, rows), lambda i, s: (unit, 0)),
            scratch_shapes=[
                pltpu.VMEM((4, EXT, old + rows), jnp.bfloat16),
                pltpu.VMEM((2, EXT, rows), jnp.bfloat16),
            ],
        ),
        out_shape=jax.ShapeDtypeStruct(output.shape, jnp.bfloat16),
        input_output_aliases={9: 0},
        compiler_params=pltpu.CompilerParams(vmem_limit_bytes=VMEM),
        cost_estimate=pl.CostEstimate(
            flops=work * 1024, bytes_accessed=5000000, transcendentals=work
        ),
        name="attend_last",
    )(scalars, arrived, bias, queries, new_cache, own, own, other, other, output)


def merge_body(slots, vision_ref, gain_ref, weight_ref, out_ref, total, *, rows_here, width):
    step = pl.program_id(0)
    floats = vision_ref[0].astype(jnp.float32)
    average = jnp.sum(floats, axis=1, keepdims=True) / D
    spread = jnp.sum(floats * floats, axis=1, keepdims=True) / D - average * average
    normed = ((floats - average) * lax.rsqrt(spread + 1e-06) * gain_ref[...].reshape(1, width)).astype(jnp.bfloat16)
    product = jnp.dot(normed, weight_ref[0], preferred_element_type=jnp.float32)

    @pl.when(step == 0)
    def _():
        total[...] = product

    @pl.when(step > 0)
    def _():
        total[...] += product

    @pl.when(step == pl.num_programs(0) - 1)
    def _():
        devices, piece_rows = out_ref.shape[:2]
        groups = total.shape[0]
        pieces = groups // piece_rows
        shape = (devices * piece_rows, groups)
        row = lax.broadcasted_iota(jnp.int32, shape, 0)
        column = lax.broadcasted_iota(jnp.int32, shape, 1)
        label_row = lax.broadcasted_iota(jnp.int32, (groups, LANES), 0) // piece_rows
        target = jnp.zeros(shape, jnp.int32)
        label = jnp.zeros(label_row.shape, jnp.float32)
        for j in range(pieces):
            target = jnp.where(column // piece_rows == j, slots[j] // rows_here, target)
            place = (slots[j] % rows_here // piece_rows + 1).astype(jnp.float32)
            label = jnp.where(label_row == j, place, label)
        hit = (target == row // piece_rows) & (column % piece_rows == row % piece_rows)
        select = jnp.where(hit, 1.0, 0.0).astype(jnp.bfloat16)
        wide = jnp.concatenate([total[...].astype(jnp.bfloat16), label.astype(jnp.bfloat16)], axis=1)
        sent = jnp.dot(select, wide, preferred_element_type=jnp.float32).astype(jnp.bfloat16)
        for w in range(devices):
            out_ref[w] = sent[w * piece_rows : (w + 1) * piece_rows]


def merge_rows(vision, ln_gain, merge_proj, image_slot, rows_here):
    parts, width, groups = vision.shape
    devices = lax.axis_size("blk")
    piece_rows = groups // image_slot.shape[0]
    return pl.pallas_call(
        functools.partial(merge_body, rows_here=rows_here, width=width),
        grid_spec=pltpu.PrefetchScalarGridSpec(
            num_scalar_prefetch=1,
            grid=(parts,),
            in_specs=[
                pl.BlockSpec((1, groups, width), lambda i, s: (i, 0, 0)),
                pl.BlockSpec((width,), lambda i, s: (0,)),
                pl.BlockSpec((1, width, width), lambda i, s: (i, 0, 0)),
            ],
            out_specs=pl.BlockSpec((devices, piece_rows, width + LANES), lambda i, s: (0, 0, 0)),
            scratch_shapes=[pltpu.VMEM((groups, width), jnp.float32)],
        ),
        out_shape=jax.ShapeDtypeStruct((devices, piece_rows, width + LANES), jnp.bfloat16),
        compiler_params=pltpu.CompilerParams(vmem_limit_bytes=VMEM),
        cost_estimate=pl.CostEstimate(
            flops=2 * groups * parts * width * width,
            bytes_accessed=2 * parts * width * width,
            transcendentals=0,
        ),
        name="merge_pieces",
    )(image_slot, jnp.transpose(vision, (0, 2, 1)), ln_gain, merge_proj)


def place_and_norm(arrived, text, rms_gain):
    width, rows_here = text.shape
    devices, piece_rows = arrived.shape[:2]
    lines = jnp.arange(rows_here, dtype=jnp.int32)
    offsets = jnp.arange(piece_rows, dtype=jnp.int32)
    starts = (arrived[:, 0, width].astype(jnp.int32) - 1) * piece_rows
    row_ids = (starts[:, None] + offsets[None, :]).reshape(-1)
    present = jnp.repeat(starts >= 0, piece_rows)
    hits = (row_ids[:, None] == lines[None, :]) & present[:, None]
    placed_rows = jnp.einsum(
        "kl,kr->lr",
        arrived[:, :, :width].reshape(devices * piece_rows, width),
        hits.astype(jnp.bfloat16),
        preferred_element_type=jnp.float32,
    ).astype(jnp.bfloat16)
    covered = jnp.any(hits, axis=0)
    placed = jnp.where(covered[None, :], placed_rows, text)
    row_floats = placed.astype(jnp.float32)
    square_sums = jnp.sum(row_floats * row_floats, axis=0)
    return (row_floats * lax.rsqrt(square_sums / D + 1e-06)[None, :] * rms_gain[:, None]).astype(
        jnp.bfloat16
    )


def rotary_tables(places):
    half = HD // 2
    freq_index = jnp.arange(half, dtype=jnp.float32)
    inverse = jnp.exp(freq_index * (-2.0 * math.log(10000.0) / HD))
    angles = inverse[:, None] * places[None, :]
    cosine = jnp.cos(angles)
    sine = jnp.sin(angles)
    return jnp.concatenate([cosine, cosine], axis=0), jnp.concatenate([-sine, sine], axis=0)


def swap(x, bit):
    size = lax.axis_size("blk")
    return lax.ppermute(x, "blk", [(i, i ^ (1 << bit)) for i in range(size)])


def spread_shards(
    vision, ln_gain, merge_proj, image_slot, text, rms_gain, wqkv, pcache, block_table, cache_len
):
    devices = lax.axis_size("blk")
    here = lax.axis_index("blk")
    width, rows = text.shape
    pairs = width // PAIR
    owned = pcache.shape[2] // BS
    table_width = block_table.shape[1]
    each = table_width // devices

    tie = lax.optimization_barrier
    outbound = merge_rows(vision, ln_gain, merge_proj, image_slot, rows)
    outbound, block_table = tie((outbound, block_table))
    holder = jnp.where(block_table >= 0, block_table // owned, -1)
    local = block_table - here * owned
    mine = holder == here
    longest = jnp.argmax(block_table[:, table_width - 1]).astype(jnp.int32)
    chosen = jnp.max(jnp.where(mine, local, 0), axis=1)
    star_row = jnp.where(
        lax.dynamic_index_in_dim(mine, longest, 0, False),
        lax.dynamic_index_in_dim(local, longest, 0, False),
        -1,
    )
    rank = jnp.sum((star_row[None, :] > star_row[:, None]).astype(jnp.int32), axis=1)
    star_ids = jnp.sum(
        jnp.where(
            (rank[None, :] == jnp.arange(each, dtype=jnp.int32)[:, None]) & (star_row >= 0)[None, :],
            star_row[None, :],
            0,
        ),
        axis=1,
    )
    row_holder = lax.dynamic_index_in_dim(holder, here, 0, False)
    row_count = jnp.clip(cache_len[0] - BS * jnp.arange(table_width, dtype=jnp.int32), 0, BS)
    live = jnp.sum(
        jnp.where(
            row_holder[None, :] == jnp.arange(devices, dtype=jnp.int32)[:, None], row_count[None, :], 0
        ),
        axis=1,
    )
    live = jnp.where(here == longest, 0, live)
    bias = jnp.where(jnp.arange(BS, dtype=jnp.int32)[None, :] < live[:, None], 0.0, MASKED)
    bias = bias.astype(jnp.float32).reshape(1, devices * BS)

    paged = pcache.reshape(2, pairs, PAIR, owned * BS)
    units = pairs // 2

    def exchange(x):
        return lax.all_to_all(x, "blk", split_axis=0, concat_axis=0, tiled=True)

    pieces_in = exchange(outbound)
    head = units - 1
    packed = pack_units(chosen, paged, 0, head)
    packed, pieces_in = tie((packed, pieces_in))
    arrived = exchange(packed)
    packed_last = pack_units(chosen, paged, head, units - head)

    normed = place_and_norm(pieces_in, text, rms_gain)
    normed, packed_last = tie((normed, packed_last))
    places = (cache_len[0] + jnp.arange(rows, dtype=jnp.int32)).astype(jnp.float32)
    tables = rotary_tables(places)
    queries = project(normed, wqkv, *tables, (0,))

    plane_bits = pairs.bit_length() - 1
    all_bits = devices.bit_length() - 1
    place = here % pairs
    pair = place % 2 * 4 + place // 2 % 2 * 2 + place // 4
    query = queries
    for bit in range(plane_bits):
        mine_bit, star_bit = (here >> bit) & 1, (longest >> bit) & 1
        halves = query.reshape(2, query.shape[0] // 2, PAIR, rows)
        kept = lax.dynamic_index_in_dim(halves, mine_bit, 0, False)
        given = lax.dynamic_index_in_dim(halves, 1 - mine_bit, 0, False)
        taken = swap(given, bit)
        if bit == 0:
            normed, taken = tie((normed, taken))
            new_cache = project(normed, wqkv, *tables, (1, 2))
        if bit == 1:
            taken, new_cache = tie((taken, new_cache))
            star_ids, taken = tie((star_ids, taken))
            star_ids = jnp.concatenate([pair.astype(jnp.int32).reshape(1), star_ids])
            star_kv = star_pack(star_ids, paged)
        if bit == 2:
            taken, star_kv = tie((taken, star_kv))
            star_parts = [star_kv[0:1]]
            for i in range(1, pairs):
                away = i % 2 * 4 + i // 2 % 2 * 2 + i // 4
                star_parts.append(
                    lax.ppermute(star_kv[i : i + 1], "blk", [(d, d ^ away) for d in range(devices)])
                )
        query = jnp.where(star_bit == mine_bit, kept, taken)
    for bit in range(plane_bits, all_bits):
        same = ((here ^ longest) >> bit) & 1
        query = jnp.where(same == 0, query, swap(query, bit))
    star_parts, query = tie((star_parts, query))
    star = star_attend(star_parts, query)
    results = []
    came = [arrived]

    def attend_next(*after):
        u = len(results)
        held, *_ = tie((bias, *after))
        chunk, place = (came[0], u) if u < head else (came[1], u - head)
        results.append(attend_unit(chunk, place, held, queries, new_cache, u))

    half = pairs // 2
    mates = [i % 2 * 4 + i // 2 % 2 * 2 + i // 4 for i in range(half)]
    for bit in range(plane_bits, all_bits):
        other = swap(star, bit)
        if bit == all_bits - 1:
            attend_next(star)
            other, results = tie((other, results))
            packed_last, came[0], other = tie((packed_last, came[0], other))
            came.append(exchange(packed_last))
        star = fold(star, other)
    own = [star]
    for away in mates[1:]:
        own.append(lax.ppermute(star, "blk", [(d, d ^ away) for d in range(devices)]))
    while len(results) < head:
        attend_next(star)
    own, results = tie((own, results))
    own = jnp.stack(own)
    other = swap(own, 0)
    scalars = jnp.stack([(here == longest).astype(jnp.int32), pair.astype(jnp.int32)])
    output = finish(scalars, own, other, results)
    output, came[1] = tie((output, came[1]))
    output = attend_last(scalars, came[1], bias, queries, new_cache, own, other, output, head)
    return (output, new_cache)


def spreads(mesh):
    devices = mesh.shape["blk"]
    pairs = D // PAIR
    return mesh.shape["head"] == 1 and devices % pairs == 0 and devices & (devices - 1) == 0


def solution(mesh):
    in_specs = (
        P(None, "head", "blk"),
        P("head"),
        P(None, "head", None),
        P("blk"),
        P("head", "blk"),
        P(),
        P(None, "head", None),
        P(None, "head", "blk"),
        P(),
        P("blk"),
    )
    out_specs = (P("head", "blk"), P(None, "head", "blk"))
    body = spread_shards if spreads(mesh) else shards
    return jax.shard_map(body, mesh=mesh, in_specs=in_specs, out_specs=out_specs, check_vma=False)
```
